512 devices in a mesh: layer: 8 (over y, core), uvrow: 64 (over z, x).
Axes of the slice: x: 4, y: 4, z: 16, core: 2. Of those that a mesh axis runs over, the one named last changes fastest.
Arguments:
- vis_values: float32 [32768, 2, 128], P(('layer', 'uvrow')), may hold values from -6 to 6
- vis_cell: int32 [32768, 128], P(('layer', 'uvrow')), may hold values from 0 to 3871
- vis_offset: int32 [32768, 128], P(('layer', 'uvrow')), may hold values from 0 to 63
- block_tile: int32 [32768, 1], P(('layer', 'uvrow')), may hold values from 0 to 15
- block_band: int32 [32768, 1], P(('layer', 'uvrow')), may hold values from 0 to 63; in each aligned block of 64 rows (0 to 63, 64 to 127, ...) at most 2 rows name the same one
- layer_w: float32 [8], replicated, may hold values from -300 to 300
Outputs:
- dirty_map: float32 [2048, 2048], P(('layer', 'uvrow'))
The draws below stay inside these ranges and needn't reach their ends.
Inputs may be any that keep to these rules, and one draw needn't show every extreme that they name: `block_band`: among the 64 blocks of one device no band is named more than 2 times, and in every draw some device names some band exactly 2 times.
All inputs are finite; a program needn't handle non-finite values.
Results may differ from the reference program's by a relative error of at most 0.0003.
Values sent between devices are 32-bit elements; how exact they have to be, the bound alone decides.
A program may use at most 64 MiB of HBM per device.

```python
import math
import jax
import jax.numpy as jnp
import numpy as np
from jax import lax

N = 2048
TW = 128
K = 8
OVS = 8
VB = 128
BLK_DEV = 64
CAP = 2
LAYERS = 8
BAND_ROWS = 32
LAYER_BLOCKS = 4096
BLOCKS = 32768
N_UVROW = 64


def plant(entries, stream_key, least, largest):
    longest = entries.shape.index(max(entries.shape))
    spots = []
    for shift in (0, 1):
        where = [jax.random.randint(jax.random.fold_in(stream_key, axis), (), 0, length) for axis, length in enumerate(entries.shape)]
        where[longest] = (where[longest] + shift) % entries.shape[longest]
        spots.append(tuple(where))
    return entries.at[spots[0]].set(least).at[spots[1]].set(largest)


def block_levels(rng, shape, shards, smallest, high):
    loudness = 1.0
    for position, parts in shards:
        steps = jax.random.uniform(jax.random.fold_in(jax.random.fold_in(rng, 6), position), (parts,), jnp.float32, smallest / len(shards), high / len(shards))
        loudness = loudness * jnp.repeat(jnp.exp(steps), shape[position] // parts).reshape((-1,) + (1,) * (len(shape) - 1 - position))
    return loudness


def assign_block(own_key, own, number, rows, count, top, most, slope):
    order = jax.random.permutation(own_key, count)
    heavy_load, usual = portions_of(count, rows * top, most, slope, True), portions_of(count, rows * top, most, slope, False)
    places = jnp.arange(count)

    def named(lengths, offset_by):
        used = int((lengths > 0).sum())
        fixed = max(1, used // 4)
        passed = fixed + (places - fixed + offset_by * (used - fixed)) % max(1, count - fixed)
        return jnp.zeros((count,), jnp.int32).at[order[jnp.where(places < fixed, places, passed)]].set(jnp.asarray(lengths, jnp.int32))

    lengths = jnp.where(number % 4 == 0, named(heavy_load, number // 4), named(usual, number - number // 4 - 1))
    mixed = jax.random.permutation(jax.random.fold_in(own, 3), count)
    donor, sink = mixed[0:count // 2 * 2:2], mixed[1:count // 2 * 2:2]
    slack = jnp.minimum(lengths[donor] - 1, most - lengths[sink]) // 2
    slack = jnp.where((donor == order[0]) | (sink == order[0]) | (lengths[sink] == 0), 0, jnp.maximum(slack, 0))
    passed = jax.random.randint(jax.random.fold_in(own, 4), (count // 2,), 0, 1 << 20) % (slack + 1)
    lengths = lengths.at[donor].add(-passed).at[sink].add(passed)
    members = jnp.searchsorted(jnp.cumsum(lengths), jnp.arange(rows * top), side="right").astype(jnp.int32)
    table = members.reshape(top, rows).T
    table = table[jax.random.permutation(jax.random.fold_in(own, 1), rows)]
    offset_by = jax.random.randint(jax.random.fold_in(own, 2), (rows, 1), 0, top)
    return jnp.take_along_axis(table, (jnp.arange(top)[None, :] + offset_by) % top, axis=1)


def portions_of(amount, total, reach, slope, full):
    weights = [(1 << 20) // math.isqrt(rank ** slope) + 1 for rank in range(1, amount + 1)]
    largest = reach if full else min(reach, max(-(-total // amount), total * weights[0] // sum(weights)))
    least = 1 if total - largest >= amount - 1 else 0
    given, rest = [largest] + [least] * (amount - 1), total - largest - least * (amount - 1)
    while rest > 0:
        candidates = [i for i in range(1, amount) if given[i] < largest] or [i for i in range(1, amount) if given[i] < reach]
        pool, left = sum([weights[i] for i in candidates]), rest
        for i in candidates:
            extra = min(reach - given[i], max(1, left * weights[i] // pool), rest)
            given[i] = given[i] + extra
            rest = rest - extra
    return np.array(given)


def bell_draw(stream_key, dims, width, reach, cuts=(), held_as=jnp.bfloat16):
    array = jax.random.normal(stream_key, dims, jnp.float32) * width
    if len(cuts) > 0:
        array = block_levels(stream_key, dims, cuts, -0.22, 0.18) * array
    return jnp.clip(array, min=-reach, max=reach).astype(held_as)


def setup_inputs(seed: int = 0) -> dict:
    streams_of = jax.random.split(jax.random.key(seed), 7)
    vis_values = bell_draw(streams_of[0], (BLOCKS, 2, VB), 1.0, 6.0, ((0, 512),), jnp.float32)
    vis_cell = plant(jax.random.randint(streams_of[1], (BLOCKS, VB), 0, (N // N_UVROW) * (TW - K + 1)), jax.random.fold_in(streams_of[1], 1), 0, ((N // N_UVROW) * (TW - K + 1)) - 1).astype(jnp.int32)
    vis_offset = plant(jax.random.randint(streams_of[2], (BLOCKS, VB), 0, OVS * OVS), jax.random.fold_in(streams_of[2], 1), 0, (OVS * OVS) - 1).astype(jnp.int32)
    block_tile = plant(jax.random.randint(streams_of[3], (BLOCKS, 1), 0, N // TW), jax.random.fold_in(streams_of[3], 1), 0, (N // TW) - 1).astype(jnp.int32)
    block_band_keys = jax.random.split(jax.random.fold_in(streams_of[4], 1), BLOCKS // BLK_DEV)
    block_band_turns = jax.random.permutation(jax.random.fold_in(streams_of[4], 3), BLOCKS // BLK_DEV)
    block_band = jax.vmap(lambda own, number: assign_block(jax.random.fold_in(streams_of[4], 2), own, number, BLK_DEV, N_UVROW, 1, CAP, 2))(block_band_keys, block_band_turns).reshape((BLOCKS, 1))
    layer_w = jnp.clip(jax.random.uniform(streams_of[5], (LAYERS,), jnp.float32, -300.0, 300.0), -300.0, 300.0)
    return {"vis_values": vis_values, "vis_cell": vis_cell, "vis_offset": vis_offset, "block_tile": block_tile, "block_band": block_band, "layer_w": layer_w}


KERNEL_SIGMA = 1.45
FIELD_WIDTH = 0.6

def kernel_taps(distance, fraction, support):
    centre = (support - 1) / 2.0
    inside = (distance >= 0) & (distance < support)
    offset = distance.astype(jnp.float32) - centre - fraction
    values = jnp.exp(-(offset * offset) / (2.0 * KERNEL_SIGMA * KERNEL_SIGMA))
    return jnp.where(inside, values, 0.0)

def screen_phase(pixel_rows, pixel_cols, layer_depth, length):
    half_length = length // 2
    first_coord = ((pixel_rows + half_length) % length - half_length).astype(jnp.float32) * (FIELD_WIDTH / length)
    second_coord = ((pixel_cols + half_length) % length - half_length).astype(jnp.float32) * (FIELD_WIDTH / length)
    radius = first_coord[..., None] * first_coord[..., None] + second_coord * second_coord
    depth_term = -radius / (1.0 + jnp.sqrt(1.0 - radius))
    return 2.0 * math.pi * layer_depth * depth_term

def reference(vis_values, vis_cell, vis_offset, block_tile, block_band, layer_w):
    col_span = TW - K + 1
    norm_scale = 1.0 / math.sqrt(BLOCKS * VB)
    tap_ids = jnp.arange(K, dtype=jnp.int32)
    row_table = kernel_taps(tap_ids[:, None], jnp.arange(OVS, dtype=jnp.int32).astype(jnp.float32)[None, :] / OVS, K)
    pixel_ids = jnp.arange(N, dtype=jnp.int32)

    def one_layer(running, layer):
        first_block = layer * LAYER_BLOCKS
        values = lax.dynamic_slice_in_dim(vis_values, first_block, LAYER_BLOCKS, 0)
        cell_ids = lax.dynamic_slice_in_dim(vis_cell, first_block, LAYER_BLOCKS, 0)
        offsets = lax.dynamic_slice_in_dim(vis_offset, first_block, LAYER_BLOCKS, 0)
        tile_ids = lax.dynamic_slice_in_dim(block_tile, first_block, LAYER_BLOCKS, 0)
        band_ids = lax.dynamic_slice_in_dim(block_band, first_block, LAYER_BLOCKS, 0)
        grid_row = band_ids * BAND_ROWS + cell_ids // col_span
        grid_col = tile_ids * TW + cell_ids % col_span
        row_plane = offsets // OVS
        col_frac = (offsets % OVS).astype(jnp.float32) / OVS
        column_kernel_taps = kernel_taps(tap_ids[None, None, :], col_frac[:, :, None], K)
        flat_index = ((row_plane * N + grid_row) * N + grid_col)[:, :, None] + tap_ids[None, None, :]
        flat_index = flat_index.reshape(-1).astype(jnp.int32)
        spread_re = (values[:, 0, :, None] * column_kernel_taps).reshape(-1)
        spread_im = (values[:, 1, :, None] * column_kernel_taps).reshape(-1)
        held_re = jnp.zeros((OVS * N * N,), jnp.float32).at[flat_index].add(spread_re).reshape(OVS, N, N)
        held_im = jnp.zeros((OVS * N * N,), jnp.float32).at[flat_index].add(spread_im).reshape(OVS, N, N)
        grid_re = jnp.zeros((N, N), jnp.float32)
        grid_im = jnp.zeros((N, N), jnp.float32)
        for tap_index in range(K):
            grid_re = grid_re + jnp.roll(jnp.einsum('d,dun->un', row_table[tap_index], held_re, precision=lax.Precision.HIGHEST), tap_index, axis=0)
            grid_im = grid_im + jnp.roll(jnp.einsum('d,dun->un', row_table[tap_index], held_im, precision=lax.Precision.HIGHEST), tap_index, axis=0)
        spectrum = jnp.fft.ifft2(grid_re + 1j * grid_im) * (N * N)
        image_re = jnp.real(spectrum).T
        image_im = jnp.imag(spectrum).T
        phases = screen_phase(pixel_ids, pixel_ids, layer_w[layer], N)
        layer_term = (image_re * jnp.cos(phases) - image_im * jnp.sin(phases)) * norm_scale
        return (running + layer_term, None)
    dirty_map = lax.scan(one_layer, jnp.zeros((N, N), jnp.float32), jnp.arange(LAYERS, dtype=jnp.int32))[0]
    return dirty_map
```

```python
import functools
import math

import jax
import jax.numpy as jnp
import ml_dtypes
import numpy as np
from jax import lax
from jax.experimental import pallas as pl
from jax.experimental.pallas import tpu as pltpu
from jax.sharding import PartitionSpec as P

N = 2048
TW = 128
K = 8
SPAN = TW - K + 1
BANDS = 64
LAYERS = 8
BLOCKS = 64
ROWS = 32
EXT = 40
SIGMA = 1.45
WIDTH = 0.6
TAP_SCALE = math.sqrt(math.log2(math.e) / (2.0 * SIGMA * SIGMA))
MESH = pl.DeviceIdType.MESH
F32 = jnp.float32
BF16 = jnp.bfloat16
NN = (((1,), (0,)), ((), ()))
NT = (((1,), (1,)), ((), ()))


def halves(x):
    high = x.astype(BF16)
    low = (x - high.astype(F32)).astype(BF16)
    return high, low


def host_halves(x):
    high = x.astype(np.float32).astype(ml_dtypes.bfloat16)
    low = (x - high.astype(np.float64)).astype(np.float32).astype(ml_dtypes.bfloat16)
    return high, low


def host_tables():
    p1 = np.array([16 * k + z for z in range(16) for k in range(8)])
    col = np.arange(TW)
    angle = 2 * np.pi * ((p1[:, None] * col[None, :]) % TW) / TW
    high, low = host_halves(np.concatenate([np.cos(angle), np.sin(angle)], axis=1))
    outer = np.concatenate([high, high, low], axis=1)
    angle = 2 * np.pi * (np.arange(16)[:, None] * col[None, :]) / N
    twist = np.stack([np.cos(angle), np.sin(angle)]).astype(np.float32)
    q0 = np.arange(64)
    angle = 2 * np.pi * ((q0[:, None] * q0[None, :]) % 64) / 64
    high, low = host_halves(np.concatenate([np.cos(angle), np.sin(angle)], axis=0))
    bands = np.concatenate([high, high, low], axis=1)
    r = np.arange(ROWS)
    angle = 2 * np.pi * (q0[:, None] * r[None, :]) / N
    cos, sin = np.cos(angle), np.sin(angle)
    turn = np.stack(
        [np.concatenate([cos, -sin] * 2, axis=1), np.concatenate([sin, cos] * 2, axis=1)]
    ).astype(np.float32)
    angle = 2 * np.pi * ((r[:, None] * r[None, :]) % ROWS) / ROWS
    cos, sin = np.cos(angle), np.sin(angle)
    last = np.zeros((2, 2, 2, 2, ROWS, 2, 4, ROWS))
    for ih in range(2):
        for il in range(2):
            for c in range(2):
                last[ih, 0, il, c, :, 0, 2 * ih + il, :] = cos
                last[ih, 0, il, c, :, 1, 2 * ih + il, :] = sin
                last[ih, 1, il, c, :, 0, 2 * ih + il, :] = -sin
                last[ih, 1, il, c, :, 1, 2 * ih + il, :] = cos
    high, low = host_halves(last.reshape(2, 256, 256))
    final = np.concatenate([high, high, low], axis=1)
    return outer, twist, bands, turn, final


def cos_sin_turns(turns):
    quarters = turns * 4.0
    whole = jnp.round(quarters)
    t = (quarters - whole) * (math.pi / 2)
    s = t * t
    sin = t + t * s * (-1.6666654611e-1 + s * (8.3321608736e-3 - s * 1.9515295891e-4))
    cos = 1.0 - 0.5 * s + s * s * (4.166664568298827e-2 + s * (-1.388731625493765e-3 + s * 2.443315711809948e-5))
    n = whole.astype(jnp.int32)
    odd = (n & 1) == 1
    a = jnp.where(odd, sin, cos)
    b = jnp.where(odd, cos, sin)
    a = jnp.where(((n + 1) & 2) == 2, -a, a)
    b = jnp.where((n & 2) == 2, -b, b)
    return a, b


def wrapped(pixel):
    return (((pixel + N // 2) & (N - 1)) - N // 2).astype(F32) * (WIDTH / N)


def kernel(
    values, cell, offset, tile, band, depth_ref,
    outer, twist, bands, turn, final, out,
    vis_send, vis_recv, parts, tiles, spec, spill, col_send, col_recv, screen, red_send, red_recv,
    vis_ssem, vis_rsem, spill_ssem, spill_rsem, col_ssem, col_rsem, red_ssem, red_rsem,
):
    g, w = lax.axis_index("layer"), lax.axis_index("uvrow")
    z, x = w >> 2, w & 3

    barrier = pltpu.get_barrier_semaphore()

    @pl.loop(1, BANDS)
    def _(i):
        pl.semaphore_signal(barrier, inc=1, device_id={"layer": g, "uvrow": w ^ i}, device_id_type=MESH)

    @pl.loop(1, LAYERS)
    def _(i):
        pl.semaphore_signal(barrier, inc=1, device_id={"layer": g ^ i, "uvrow": w}, device_id_type=MESH)

    row_id = lax.broadcasted_iota(jnp.int32, (BLOCKS, BLOCKS), 0)
    col_id = lax.broadcasted_iota(jnp.int32, (BLOCKS, BLOCKS), 1)
    own = jnp.broadcast_to(band[...], (BLOCKS, BLOCKS))
    other = jnp.sum(jnp.where(row_id == col_id, own, 0), axis=0, keepdims=True)
    same = own == other
    rank = jnp.sum(jnp.where(same & (row_id < col_id), 1, 0), axis=0, keepdims=True)
    cells = cell[...].astype(F32)
    rows = jnp.floor((cells + 0.5) * (1.0 / SPAN))
    cols = cells - rows * SPAN
    shifts = offset[...]
    u_place = rows * 8.0 + (shifts >> 3).astype(F32)
    v_place = (cols + tile[...].astype(F32) * TW) * 8.0 + (shifts & 7).astype(F32)
    data = jnp.concatenate([values[:, 0, :], values[:, 1, :], u_place, v_place], axis=1)
    first = data.astype(BF16)
    rest = data - first.astype(F32)
    second = rest.astype(BF16)
    third = (rest - second.astype(F32)).astype(BF16)
    stacked = jnp.concatenate([first, second, third], axis=0)
    for j in range(2):
        pick = jnp.where((row_id == other) & (rank == j), 1.0, 0.0).astype(BF16)
        pick = jnp.concatenate([pick, pick, pick], axis=1)
        slots = lax.dot_general(pick, stacked, NN, preferred_element_type=F32)
        for f in range(4):
            vis_send[pl.ds(4 * j + f, BANDS, stride=8), :] = slots[:, f * 128 : (f + 1) * 128]

    depth = depth_ref[g]
    lane = lax.broadcasted_iota(jnp.int32, (64, 128), 1)
    y = wrapped((lane & 31) * 64 + lax.broadcasted_iota(jnp.int32, (64, 128), 0))

    @pl.loop(0, LAYERS)
    def _(k):
        xp = wrapped(256 * k + 4 * w + (lane >> 5))
        r = xp * xp + y * y
        turns = depth * (-r / (1.0 + jnp.sqrt(1.0 - r)))
        cos, sin = cos_sin_turns(turns)
        screen[k, 0] = cos * (1.0 / N)
        screen[k, 1] = sin * (1.0 / N)

    pl.semaphore_wait(barrier, BANDS - 1 + LAYERS - 1)

    def vis_copy(i):
        there = w ^ i
        return pltpu.make_async_remote_copy(
            src_ref=vis_send.at[pl.ds(pl.multiple_of(there * 8, 8), 8)],
            dst_ref=vis_recv.at[pl.ds(pl.multiple_of(w * 8, 8), 8)],
            send_sem=vis_ssem,
            recv_sem=vis_rsem.at[i],
            device_id={"layer": g, "uvrow": there},
            device_id_type=MESH,
        )

    @pl.loop(1, BANDS)
    def _(i):
        vis_copy(i).start()

    mine = pl.ds(pl.multiple_of(w * 8, 8), 8)
    vis_recv[mine, :] = vis_send[mine, :]

    row_axis = lax.broadcasted_iota(jnp.int32, (EXT, 128), 0).astype(F32)
    col_axis = lax.broadcasted_iota(jnp.int32, (TW, 128), 0).astype(F32)

    def taps(axis, place):
        begin = jnp.floor(place * 0.125)
        far = axis * TAP_SCALE - (place * 0.125 + (K - 1) / 2.0) * TAP_SCALE
        inside = (axis >= begin) & (axis < begin + K)
        return jnp.where(inside, jnp.exp2(-(far * far)), 0.0)

    @pl.loop(0, BANDS)
    def _(i):
        there = pl.multiple_of((w ^ i) * 8, 8)

        @pl.when(i > 0)
        def _():
            piece = vis_recv.at[pl.ds(there, 8)]
            pltpu.make_async_copy(piece, piece, vis_rsem.at[i]).wait()

        message = vis_recv[pl.ds(there, 8), :]
        for j in range(2):
            v_all = message[4 * j + 3 : 4 * j + 4]
            number = jnp.floor(v_all * (1.0 / 1024))
            row_taps = taps(row_axis, message[4 * j + 2 : 4 * j + 3])
            weighted = jnp.concatenate(
                [row_taps * message[4 * j : 4 * j + 1], row_taps * message[4 * j + 1 : 4 * j + 2]], axis=0
            )
            col_taps = taps(col_axis, v_all - number * 1024.0)
            wh, wl = halves(weighted)
            ch, cl = halves(col_taps)
            patch = lax.dot_general(
                jnp.concatenate([wh, wl, wh], axis=1),
                jnp.concatenate([ch, ch, cl], axis=1),
                NT,
                preferred_element_type=F32,
            )
            parts[pl.ds(pl.multiple_of((2 * i + j) * 2 * EXT, 16), 2 * EXT), :] = patch
            tiles[pl.ds(2 * i + j, 1), :] = number

    by_slot = jnp.transpose(tiles[...])[:16]
    p0 = lax.broadcasted_iota(jnp.int32, (16, 128), 0).astype(F32)
    cos, sin = cos_sin_turns(by_slot * p0 * (1.0 / 16))
    mh, ml = halves(jnp.concatenate([cos, sin], axis=0))
    mix = jnp.concatenate([mh, mh, ml], axis=1)

    def tile_row(u):
        re = parts[pl.ds(u, 128, stride=2 * EXT), :]
        im = parts[pl.ds(u + EXT, 128, stride=2 * EXT), :]
        ph, plo = halves(jnp.concatenate([re, im], axis=1))
        both = lax.dot_general(
            mix, jnp.concatenate([ph, plo, ph], axis=0), NN, preferred_element_type=F32
        )
        re = both[:16, :128] - both[16:, 128:]
        im = both[:16, 128:] + both[16:, :128]
        tc, ts = twist[0], twist[1]
        at = pl.ds(pl.multiple_of(u * 16, 16), 16)
        spec[0, at, :] = re * tc - im * ts
        spec[1, at, :] = re * ts + im * tc

    @pl.loop(ROWS, EXT)
    def _(u):
        tile_row(u)

    after, before = (w + 1) & (BANDS - 1), (w + BANDS - 1) & (BANDS - 1)
    spill_copy = pltpu.make_async_remote_copy(
        src_ref=spec.at[:, pl.ds(ROWS * 16, (EXT - ROWS) * 16)],
        dst_ref=spill,
        send_sem=spill_ssem,
        recv_sem=spill_rsem,
        device_id={"layer": g, "uvrow": after},
        device_id_type=MESH,
    )
    spill_copy.start()

    @pl.loop(0, ROWS)
    def _(u):
        tile_row(u)

    spill_copy.wait()
    over = pl.ds(0, (EXT - ROWS) * 16)
    spec[:, over, :] = spec[:, over, :] + spill[...]

    for pair in range(8):
        there_x, ih = pair // 2, pair % 2
        operand = []
        for il in range(2):
            re = spec[0, pl.ds(2 * pair + il, ROWS, stride=16), :]
            im = spec[1, pl.ds(2 * pair + il, ROWS, stride=16), :]
            operand.append(jnp.concatenate([re, -im], axis=1))
            operand.append(jnp.concatenate([im, re], axis=1))
        oh, ol = halves(jnp.concatenate(operand, axis=0))
        half = lax.dot_general(
            outer[...], jnp.concatenate([oh, ol, oh], axis=1), NT, preferred_element_type=F32
        )
        for there_z in range(16):
            at = (4 * there_z + there_x) * 16 + 8 * ih
            col_send[at : at + 8, :] = half[8 * there_z : 8 * there_z + 8]
        if ih == 1:

            @pl.loop(0, 16)
            def _(dz):
                there = ((z ^ dz) << 2) + there_x

                @pl.when(there != w)
                def _():
                    pltpu.make_async_remote_copy(
                        src_ref=col_send.at[pl.ds(pl.multiple_of(there * 16, 16), 16)],
                        dst_ref=col_recv.at[pl.ds(pl.multiple_of(w * 16, 16), 16)],
                        send_sem=col_ssem,
                        recv_sem=col_rsem,
                        device_id={"layer": g, "uvrow": there},
                        device_id_type=MESH,
                    ).start()

    mine = pl.ds(pl.multiple_of(w * 16, 16), 16)
    col_recv[mine, :] = col_send[mine, :]
    others = col_recv.at[pl.ds(0, (BANDS - 1) * 16)]
    pltpu.make_async_copy(others, others, col_rsem).wait()

    def term(k):
        held = jnp.concatenate(
            [col_recv[pl.ds(k, 64, stride=16), :], col_recv[pl.ds(8 + k, 64, stride=16), :]], axis=1
        )
        hh, hl = halves(held)
        both = lax.dot_general(
            bands[...], jnp.concatenate([hh, hl, hh], axis=0), NN, preferred_element_type=F32
        )
        image = jnp.zeros((64, 256), F32)
        for ih in range(2):
            a, b = both[:64, 128 * ih : 128 * ih + 128], both[64:, 128 * ih : 128 * ih + 128]
            turned = jnp.concatenate(
                [a * turn[0] - b * turn[1], a * turn[1] + b * turn[0]], axis=1
            )
            th, tl = halves(turned)
            image = image + lax.dot_general(
                jnp.concatenate([th, tl, th], axis=1), final[ih], NN, preferred_element_type=F32
            )
        return image[:, :128] * screen[k, 0] - image[:, 128:] * screen[k, 1]

    def red_copy(there):
        return pltpu.make_async_remote_copy(
            src_ref=red_send.at[there],
            dst_ref=red_recv.at[g],
            send_sem=red_ssem,
            recv_sem=red_rsem,
            device_id={"layer": there, "uvrow": w},
            device_id_type=MESH,
        )

    @pl.loop(1, LAYERS)
    def _(i):
        there = g ^ i
        red_send[there] = term(there)
        red_copy(there).start()

    red_recv[g] = term(g)
    others = red_recv.at[pl.ds(0, LAYERS - 1)]
    pltpu.make_async_copy(others, others, red_rsem).wait()
    total = red_recv[0]
    for layer in range(1, LAYERS):
        total = total + red_recv[layer]
    out[...] = jnp.transpose(total)

    sent = vis_send.at[pl.ds(0, (BANDS - 1) * 8)]
    pltpu.make_async_copy(sent, sent, vis_ssem).wait()
    sent = col_send.at[pl.ds(0, (BANDS - 1) * 16)]
    pltpu.make_async_copy(sent, sent, col_ssem).wait()
    sent = red_send.at[pl.ds(0, LAYERS - 1)]
    pltpu.make_async_copy(sent, sent, red_ssem).wait()


def per_device(vis_values, vis_cell, vis_offset, block_tile, block_band, layer_w):
    tables = [jnp.asarray(t) for t in host_tables()]
    vmem = pl.BlockSpec(memory_space=pltpu.VMEM)
    smem = pl.BlockSpec(memory_space=pltpu.SMEM)
    dma = pltpu.SemaphoreType.DMA
    image = pl.pallas_call(
        kernel,
        out_shape=jax.ShapeDtypeStruct((128, 64), F32),
        in_specs=[vmem] * 5 + [smem] + [vmem] * 5,
        out_specs=vmem,
        scratch_shapes=[
            pltpu.VMEM((BANDS * 8, 128), F32),
            pltpu.VMEM((BANDS * 8, 128), F32),
            pltpu.VMEM((128 * 2 * EXT, 128), F32),
            pltpu.VMEM((128, 128), F32),
            pltpu.VMEM((2, EXT * 16, 128), F32),
            pltpu.VMEM((2, (EXT - ROWS) * 16, 128), F32),
            pltpu.VMEM((BANDS * 16, 128), F32),
            pltpu.VMEM((BANDS * 16, 128), F32),
            pltpu.VMEM((LAYERS, 2, 64, 128), F32),
            pltpu.VMEM((LAYERS, 64, 128), F32),
            pltpu.VMEM((LAYERS, 64, 128), F32),
            dma, dma((BANDS,)), dma, dma, dma, dma, dma, dma,
        ],
        compiler_params=pltpu.CompilerParams(
            collective_id=0, has_side_effects=True, vmem_limit_bytes=40 * 1024 * 1024
        ),
    )(vis_values, vis_cell, vis_offset, block_tile, block_band, layer_w, *tables)
    return image.reshape(4, N)


def solution(mesh):
    placed = (
        P(("layer", "uvrow"), None, None),
        P(("layer", "uvrow"), None),
        P(("layer", "uvrow"), None),
        P(("layer", "uvrow"), None),
        P(("layer", "uvrow"), None),
        P(),
    )
    return jax.shard_map(
        per_device,
        mesh=mesh,
        in_specs=placed,
        out_specs=P(("layer", "uvrow"), None),
        check_vma=False,
    )
```

```python
import functools
import math

import jax
import jax.numpy as jnp
import ml_dtypes
import numpy as np
from jax import lax
from jax.experimental import pallas as pl
from jax.experimental.pallas import tpu as pltpu
from jax.sharding import PartitionSpec as P

N = 2048
TW = 128
K = 8
SPAN = TW - K + 1
BANDS = 64
LAYERS = 8
BLOCKS = 64
ROWS = 32
EXT = 40
SIGMA = 1.45
WIDTH = 0.6
CHUNKS = 2
SLOTS = 2 * BANDS // CHUNKS
GROUP = 8
ROW_GROUP = 8
TAP_SCALE = math.sqrt(math.log2(math.e) / (2.0 * SIGMA * SIGMA))
MESH = pl.DeviceIdType.MESH
F32 = jnp.float32
BF16 = jnp.bfloat16
NN = (((1,), (0,)), ((), ()))
NT = (((1,), (1,)), ((), ()))

def halves(x):
    high = x.astype(BF16)
    low = (x - high.astype(F32)).astype(BF16)
    return high, low

def host_halves(x):
    high = x.astype(np.float32).astype(ml_dtypes.bfloat16)
    low = (x - high.astype(np.float64)).astype(np.float32).astype(ml_dtypes.bfloat16)
    return high, low

def host_tables():
    p1 = np.array([16 * k + z for z in range(16) for k in range(8)])
    col = np.arange(TW)
    angle = 2 * np.pi * ((p1[:, None] * col[None, :]) % TW) / TW
    high, low = host_halves(np.concatenate([np.cos(angle), np.sin(angle)], axis=1))
    outer = np.concatenate([high, high, low], axis=1)
    angle = 2 * np.pi * (np.arange(16)[:, None] * col[None, :]) / N
    twist = np.stack([np.cos(angle), np.sin(angle)]).astype(np.float32)
    q0 = np.arange(64)
    angle = 2 * np.pi * ((q0[:, None] * q0[None, :]) % 64) / 64
    high, low = host_halves(np.concatenate([np.cos(angle), np.sin(angle)], axis=0))
    bands = np.concatenate([high, high, low], axis=1)
    r = np.arange(ROWS)
    angle = 2 * np.pi * (q0[:, None] * r[None, :]) / N
    cos, sin = np.cos(angle), np.sin(angle)
    turn = np.stack(
        [np.concatenate([cos, -sin] * 2, axis=1), np.concatenate([sin, cos] * 2, axis=1)]
    ).astype(np.float32)
    angle = 2 * np.pi * ((r[:, None] * r[None, :]) % ROWS) / ROWS
    cos, sin = np.cos(angle), np.sin(angle)
    last = np.zeros((2, 2, 2, 2, ROWS, 2, 4, ROWS))
    for ih in range(2):
        for il in range(2):
            for c in range(2):
                last[ih, 0, il, c, :, 0, 2 * ih + il, :] = cos
                last[ih, 0, il, c, :, 1, 2 * ih + il, :] = sin
                last[ih, 1, il, c, :, 0, 2 * ih + il, :] = -sin
                last[ih, 1, il, c, :, 1, 2 * ih + il, :] = cos
    high, low = host_halves(last.reshape(2, 256, 256))
    final = np.concatenate([high, high, low], axis=1)
    return outer, twist, bands, turn, final

def cos_sin_turns(turns):
    quarters = turns * 4.0
    whole = jnp.round(quarters)
    t = (quarters - whole) * (math.pi / 2)
    s = t * t
    sin = t + t * s * (-1.6666654611e-1 + s * (8.3321608736e-3 - s * 1.9515295891e-4))
    cos = 1.0 - 0.5 * s + s * s * (4.166664568298827e-2 + s * (-1.388731625493765e-3 + s * 2.443315711809948e-5))
    n = whole.astype(jnp.int32)
    odd = (n & 1) == 1
    a = jnp.where(odd, sin, cos)
    b = jnp.where(odd, cos, sin)
    a = jnp.where(((n + 1) & 2) == 2, -a, a)
    b = jnp.where((n & 2) == 2, -b, b)
    return a, b

def wrapped(pixel):
    return (((pixel + N // 2) & (N - 1)) - N // 2).astype(F32) * (WIDTH / N)

def kernel(
    values_hbm, cell_hbm, offset_hbm, tile_hbm, band_hbm, depth_hbm,
    outer_hbm, twist_hbm, bands_hbm, turn_hbm, final_hbm, out,
    values, cell, offset, tile, band, depth_ref, outer, twist, bands, turn, final,
    vis_send, vis_recv, parts, tiles, spec, spill, col_send, col_recv, screen, red_send, red_recv,
    load_sem, vis_ssem, vis_rsem, spill_ssem, spill_rsem, col_ssem, col_rsem, red_ssem, red_rsem,
):
    g, w = lax.axis_index("layer"), lax.axis_index("uvrow")
    z, x = w >> 2, w & 3

    barrier = pltpu.get_barrier_semaphore()
    loads = [
        pltpu.make_async_copy(there, here, load_sem.at[n])
        for n, (there, here) in enumerate(
            [
                (band_hbm, band), (tile_hbm, tile), (cell_hbm, cell), (offset_hbm, offset),
                (values_hbm, values), (depth_hbm, depth_ref), (twist_hbm, twist), (outer_hbm, outer),
                (bands_hbm, bands), (turn_hbm, turn), (final_hbm, final),
            ]
        )
    ]
    for load in loads:
        load.start()

    @pl.loop(1, BANDS)
    def _(i):
        pl.semaphore_signal(barrier, inc=1, device_id={"layer": g, "uvrow": w ^ i}, device_id_type=MESH)

    @pl.loop(1, LAYERS)
    def _(i):
        pl.semaphore_signal(barrier, inc=1, device_id={"layer": g ^ i, "uvrow": w}, device_id_type=MESH)

    for load in loads[:6]:
        load.wait()

    row_id = lax.broadcasted_iota(jnp.int32, (BLOCKS, BLOCKS), 0)
    col_id = lax.broadcasted_iota(jnp.int32, (BLOCKS, BLOCKS), 1)
    other = jnp.broadcast_to(band[...], (BLOCKS, BLOCKS))
    own = jnp.sum(jnp.where(row_id == col_id, other, 0), axis=1, keepdims=True)
    tile_of = jnp.sum(jnp.where(row_id == col_id, jnp.broadcast_to(tile[...], (BLOCKS, BLOCKS)), 0), axis=1, keepdims=True)
    same = own == other
    rank = jnp.sum(jnp.where(same & (row_id < col_id), 1, 0), axis=0, keepdims=True)
    cells = cell[...].astype(F32)
    rows = jnp.floor((cells + 0.5) * (1.0 / SPAN))
    cols = cells - rows * SPAN
    shifts = offset[...]
    u_place = rows * 8.0 + (shifts >> 3).astype(F32)
    v_place = (cols + tile_of.astype(F32) * TW) * 8.0 + (shifts & 7).astype(F32)
    data = jnp.concatenate([values[:, 0, :], values[:, 1, :], u_place, v_place], axis=1)
    first = data.astype(BF16)
    rest = data - first.astype(F32)
    second = rest.astype(BF16)
    third = (rest - second.astype(F32)).astype(BF16)
    stacked = jnp.concatenate([first, second, third], axis=0)
    for j in range(2):
        pick = jnp.where((row_id == other) & (rank == j), 1.0, 0.0).astype(BF16)
        pick = jnp.concatenate([pick, pick, pick], axis=1)
        slots = lax.dot_general(pick, stacked, NN, preferred_element_type=F32)
        for f in range(4):
            vis_send[pl.ds(4 * j + f, BANDS, stride=8), :] = slots[:, f * 128 : (f + 1) * 128]

    depth = depth_ref[g]
    lane = lax.broadcasted_iota(jnp.int32, (64, 128), 1)
    y = wrapped((lane & 31) * 64 + lax.broadcasted_iota(jnp.int32, (64, 128), 0))

    @pl.loop(0, LAYERS)
    def _(k):
        xp = wrapped(256 * k + 4 * w + (lane >> 5))
        r = xp * xp + y * y
        turns = depth * (-r / (1.0 + jnp.sqrt(1.0 - r)))
        cos, sin = cos_sin_turns(turns)
        screen[k, 0] = cos * (1.0 / N)
        screen[k, 1] = sin * (1.0 / N)

    pl.semaphore_wait(barrier, BANDS - 1 + LAYERS - 1)

    def vis_copy(i):
        there = w ^ i
        return pltpu.make_async_remote_copy(
            src_ref=vis_send.at[pl.ds(pl.multiple_of(there * 8, 8), 8)],
            dst_ref=vis_recv.at[pl.ds(pl.multiple_of(w * 8, 8), 8)],
            send_sem=vis_ssem,
            recv_sem=vis_rsem.at[i],
            device_id={"layer": g, "uvrow": there},
            device_id_type=MESH,
        )

    @pl.loop(1, BANDS)
    def _(i):
        vis_copy(i).start()

    mine = pl.ds(pl.multiple_of(w * 8, 8), 8)
    pltpu.make_async_copy(vis_send.at[mine], vis_recv.at[mine], vis_rsem.at[0]).start()
    for load in loads[6:]:
        load.wait()

    row_axis = lax.broadcasted_iota(jnp.int32, (EXT, 128), 0).astype(F32)
    col_axis = lax.broadcasted_iota(jnp.int32, (TW, 128), 0).astype(F32)

    def taps(axis, place):
        begin = jnp.floor(place * 0.125)
        far = axis * TAP_SCALE - (place * 0.125 + (K - 1) / 2.0) * TAP_SCALE
        inside = (axis >= begin) & (axis < begin + K)
        return jnp.where(inside, jnp.exp2(-(far * far)), 0.0)

    def patches(i, count):
        messages = []
        for n in range(count):
            piece = vis_recv.at[pl.ds(pl.multiple_of((w ^ (i + n)) * 8, 8), 8)]
            pltpu.make_async_copy(piece, piece, vis_rsem.at[i + n]).wait()
        for n in range(count):
            messages.append(vis_recv[pl.ds(pl.multiple_of((w ^ (i + n)) * 8, 8), 8), :])
        for n in range(count):
            message = messages[n]
            for j in range(2):
                slot = (2 * (i + n) + j) & (SLOTS - 1)
                v_all = message[4 * j + 3 : 4 * j + 4]
                number = jnp.floor(v_all * (1.0 / 1024))
                row_taps = taps(row_axis, message[4 * j + 2 : 4 * j + 3])
                weighted = jnp.concatenate(
                    [row_taps * message[4 * j : 4 * j + 1], row_taps * message[4 * j + 1 : 4 * j + 2]], axis=0
                )
                col_taps = taps(col_axis, v_all - number * 1024.0)
                wh, wl = halves(weighted)
                ch, cl = halves(col_taps)
                patch = lax.dot_general(
                    jnp.concatenate([wh, wl, wh], axis=1),
                    jnp.concatenate([ch, ch, cl], axis=1),
                    NT,
                    preferred_element_type=F32,
                )
                parts[pl.ds(pl.multiple_of(slot * 2 * EXT, 16), 2 * EXT), :] = patch
                for copy in range(3):
                    tiles[pl.ds(copy * SLOTS + slot, 1), :] = number

    p0 = lax.broadcasted_iota(jnp.int32, (16, 3 * SLOTS), 0).astype(F32)
    exact = lax.broadcasted_iota(jnp.int32, (32, 3 * SLOTS), 1) < 2 * SLOTS

    def tile_row(u, mix, begin):
        re = parts[pl.ds(u, SLOTS, stride=2 * EXT), :]
        im = parts[pl.ds(u + EXT, SLOTS, stride=2 * EXT), :]
        ph, plo = halves(jnp.concatenate([re, im], axis=1))
        both = lax.dot_general(
            mix, jnp.concatenate([ph, plo, ph], axis=0), NN, preferred_element_type=F32
        )
        re = both[:16, :128] - both[16:, 128:]
        im = both[:16, 128:] + both[16:, :128]
        tc, ts = twist[0], twist[1]
        at = pl.ds(pl.multiple_of(u * 16, 16), 16)
        new_re, new_im = re * tc - im * ts, re * ts + im * tc
        if begin:
            spec[0, at, :] = new_re
            spec[1, at, :] = new_im
        else:
            spec[0, at, :] += new_re
            spec[1, at, :] += new_im

    after = (w + 1) & (BANDS - 1)
    spill_copy = pltpu.make_async_remote_copy(
        src_ref=spec.at[:, pl.ds(ROWS * 16, (EXT - ROWS) * 16)],
        dst_ref=spill,
        send_sem=spill_ssem,
        recv_sem=spill_rsem,
        device_id={"layer": g, "uvrow": after},
        device_id_type=MESH,
    )
    for chunk in range(CHUNKS):
        start = chunk * (SLOTS // 2)

        @pl.loop(start, start + SLOTS // 2, step=GROUP)
        def _(i):
            patches(i, GROUP)

        by_slot = jnp.transpose(tiles[...])[:16, : 3 * SLOTS]
        cos, sin = cos_sin_turns(by_slot * p0 * (1.0 / 16))
        mh, ml = halves(jnp.concatenate([cos, sin], axis=0))
        mix = jnp.where(exact, mh, ml)

        @pl.loop(ROWS, EXT, step=ROW_GROUP)
        def _(u):
            for n in range(ROW_GROUP):
                tile_row(u + n, mix, chunk == 0)

        if chunk == CHUNKS - 1:
            spill_copy.start()

        @pl.loop(0, ROWS, step=ROW_GROUP)
        def _(u):
            for n in range(ROW_GROUP):
                tile_row(u + n, mix, chunk == 0)

    spill_copy.wait()
    over = pl.ds(0, (EXT - ROWS) * 16)
    spec[:, over, :] = spec[:, over, :] + spill[...]

    for pair in range(8):
        there_x, ih = pair // 2, pair % 2
        operand = []
        for il in range(2):
            re = spec[0, pl.ds(2 * pair + il, ROWS, stride=16), :]
            im = spec[1, pl.ds(2 * pair + il, ROWS, stride=16), :]
            operand.append(jnp.concatenate([re, -im], axis=1))
            operand.append(jnp.concatenate([im, re], axis=1))
        oh, ol = halves(jnp.concatenate(operand, axis=0))
        half = lax.dot_general(
            outer[...], jnp.concatenate([oh, ol, oh], axis=1), NT, preferred_element_type=F32
        )
        for there_z in range(16):
            at = (4 * there_z + there_x) * 16 + 8 * ih
            col_send[at : at + 8, :] = half[8 * there_z : 8 * there_z + 8]
        if ih == 1:

            @pl.loop(0, 16)
            def _(dz):
                there = ((z ^ dz) << 2) + there_x

                @pl.when(there != w)
                def _():
                    pltpu.make_async_remote_copy(
                        src_ref=col_send.at[pl.ds(pl.multiple_of(there * 16, 16), 16)],
                        dst_ref=col_recv.at[pl.ds(pl.multiple_of(w * 16, 16), 16)],
                        send_sem=col_ssem,
                        recv_sem=col_rsem,
                        device_id={"layer": g, "uvrow": there},
                        device_id_type=MESH,
                    ).start()

    mine = pl.ds(pl.multiple_of(w * 16, 16), 16)
    col_recv[mine, :] = col_send[mine, :]
    others = col_recv.at[pl.ds(0, (BANDS - 1) * 16)]
    pltpu.make_async_copy(others, others, col_rsem).wait()

    def term(k):
        held = jnp.concatenate(
            [col_recv[pl.ds(k, 64, stride=16), :], col_recv[pl.ds(8 + k, 64, stride=16), :]], axis=1
        )
        hh, hl = halves(held)
        both = lax.dot_general(
            bands[...], jnp.concatenate([hh, hl, hh], axis=0), NN, preferred_element_type=F32
        )
        image = jnp.zeros((64, 256), F32)
        for ih in range(2):
            a, b = both[:64, 128 * ih : 128 * ih + 128], both[64:, 128 * ih : 128 * ih + 128]
            turned = jnp.concatenate(
                [a * turn[0] - b * turn[1], a * turn[1] + b * turn[0]], axis=1
            )
            th, tl = halves(turned)
            image = image + lax.dot_general(
                jnp.concatenate([th, tl, th], axis=1), final[ih], NN, preferred_element_type=F32
            )
        return image[:, :128] * screen[k, 0] - image[:, 128:] * screen[k, 1]

    def red_copy(there):
        return pltpu.make_async_remote_copy(
            src_ref=red_send.at[there],
            dst_ref=red_recv.at[g],
            send_sem=red_ssem,
            recv_sem=red_rsem,
            device_id={"layer": there, "uvrow": w},
            device_id_type=MESH,
        )

    @pl.loop(1, LAYERS)
    def _(i):
        there = g ^ i
        red_send[there] = term(there)
        red_copy(there).start()

    red_recv[g] = term(g)
    others = red_recv.at[pl.ds(0, LAYERS - 1)]
    pltpu.make_async_copy(others, others, red_rsem).wait()
    total = red_recv[0]
    for layer in range(1, LAYERS):
        total = total + red_recv[layer]
    out[...] = jnp.transpose(total)

    sent = vis_send.at[pl.ds(0, (BANDS - 1) * 8)]
    pltpu.make_async_copy(sent, sent, vis_ssem).wait()
    sent = col_send.at[pl.ds(0, (BANDS - 1) * 16)]
    pltpu.make_async_copy(sent, sent, col_ssem).wait()
    sent = red_send.at[pl.ds(0, LAYERS - 1)]
    pltpu.make_async_copy(sent, sent, red_ssem).wait()

def per_device(vis_values, vis_cell, vis_offset, block_tile, block_band, layer_w):
    tables = [jnp.asarray(t) for t in host_tables()]
    operands = [
        vis_values, vis_cell, vis_offset, block_tile.reshape(1, BLOCKS), block_band.reshape(1, BLOCKS), layer_w, *tables,
    ]
    hbm = pl.BlockSpec(memory_space=pltpu.HBM)
    vmem = pl.BlockSpec(memory_space=pltpu.VMEM)
    dma = pltpu.SemaphoreType.DMA
    held = [(pltpu.SMEM if a is layer_w else pltpu.VMEM)(a.shape, a.dtype) for a in operands]
    image = pl.pallas_call(
        kernel,
        out_shape=jax.ShapeDtypeStruct((128, 64), F32),
        in_specs=[hbm] * len(operands),
        out_specs=vmem,
        scratch_shapes=[
            *held,
            pltpu.VMEM((BANDS * 8, 128), F32),
            pltpu.VMEM((BANDS * 8, 128), F32),
            pltpu.VMEM((SLOTS * 2 * EXT, 128), F32),
            pltpu.VMEM((max(128, 3 * SLOTS), 128), F32),
            pltpu.VMEM((2, EXT * 16, 128), F32),
            pltpu.VMEM((2, (EXT - ROWS) * 16, 128), F32),
            pltpu.VMEM((BANDS * 16, 128), F32),
            pltpu.VMEM((BANDS * 16, 128), F32),
            pltpu.VMEM((LAYERS, 2, 64, 128), F32),
            pltpu.VMEM((LAYERS, 64, 128), F32),
            pltpu.VMEM((LAYERS, 64, 128), F32),
            dma((len(operands),)), dma, dma((BANDS,)), dma, dma, dma, dma, dma, dma,
        ],
        compiler_params=pltpu.CompilerParams(
            collective_id=0, has_side_effects=True, vmem_limit_bytes=60 * 1024 * 1024
        ),
    )(*operands)
    return image.reshape(4, N)

def solution(mesh):
    placed = (
        P(("layer", "uvrow"), None, None),
        P(("layer", "uvrow"), None),
        P(("layer", "uvrow"), None),
        P(("layer", "uvrow"), None),
        P(("layer", "uvrow"), None),
        P(),
    )
    return jax.shard_map(
        per_device,
        mesh=mesh,
        in_specs=placed,
        out_specs=P(("layer", "uvrow"), None),
        check_vma=False,
    )
```

```python
import functools
import math

import jax
import jax.numpy as jnp
import ml_dtypes
import numpy as np
from jax import lax
from jax.experimental import pallas as pl
from jax.experimental.pallas import tpu as pltpu
from jax.sharding import PartitionSpec as P

N = 2048
TW = 128
K = 8
OVS = 8
SPAN = TW - K + 1
BANDS = 64
LAYERS = 8
BLOCKS = 64
ROWS = 32
EXT = 40
SIGMA = 1.45
WIDTH = 0.6
CHUNKS = 2
SLOTS = 2 * BANDS // CHUNKS
GROUP = 8
ROW_GROUP = 8
LATE = 8
TAP_SCALE = math.sqrt(math.log2(math.e) / (2.0 * SIGMA * SIGMA))
MESH = pl.DeviceIdType.MESH
F32 = jnp.float32
BF16 = jnp.bfloat16
NN = (((1,), (0,)), ((), ()))
NT = (((1,), (1,)), ((), ()))

def tier_of(w):
    return jnp.where((w & 3) == 0, 1 + (w >> 5), 0)

def far_first(n, count):
    return count // 2 + ((n + 1) >> 1) * (1 - 2 * (n & 1))

def halves(x):
    high = x.astype(BF16)
    low = (x - high.astype(F32)).astype(BF16)
    return high, low

def host_halves(x):
    high = x.astype(np.float32).astype(ml_dtypes.bfloat16)
    low = (x - high.astype(np.float64)).astype(np.float32).astype(ml_dtypes.bfloat16)
    return high, low

def host_tables():
    p1 = np.array([16 * k + z for z in range(16) for k in range(8)])
    col = np.arange(TW)
    angle = 2 * np.pi * ((p1[:, None] * col[None, :]) % TW) / TW
    high, low = host_halves(np.concatenate([np.cos(angle), np.sin(angle)], axis=1))
    outer = np.concatenate([high, high, low], axis=1)
    angle = 2 * np.pi * (np.arange(16)[:, None] * col[None, :]) / N
    twist = np.stack([np.cos(angle), np.sin(angle)]).astype(np.float32)
    q0 = np.arange(64)
    angle = 2 * np.pi * ((q0[:, None] * q0[None, :]) % 64) / 64
    high, low = host_halves(np.concatenate([np.cos(angle), np.sin(angle)], axis=0))
    bands = np.concatenate([high, high, low], axis=1)
    r = np.arange(ROWS)
    angle = 2 * np.pi * (q0[:, None] * r[None, :]) / N
    cos, sin = np.cos(angle), np.sin(angle)
    turn = np.stack(
        [np.concatenate([cos, -sin] * 2, axis=1), np.concatenate([sin, cos] * 2, axis=1)]
    ).astype(np.float32)
    angle = 2 * np.pi * ((r[:, None] * r[None, :]) % ROWS) / ROWS
    cos, sin = np.cos(angle), np.sin(angle)
    last = np.zeros((2, 2, 2, 2, ROWS, 2, 4, ROWS))
    for ih in range(2):
        for il in range(2):
            for c in range(2):
                last[ih, 0, il, c, :, 0, 2 * ih + il, :] = cos
                last[ih, 0, il, c, :, 1, 2 * ih + il, :] = sin
                last[ih, 1, il, c, :, 0, 2 * ih + il, :] = -sin
                last[ih, 1, il, c, :, 1, 2 * ih + il, :] = cos
    high, low = host_halves(last.reshape(2, 256, 256))
    final = np.concatenate([high, high, low], axis=1)
    return outer, twist, bands, turn, final

def cos_sin_turns(turns):
    quarters = turns * 4.0
    whole = jnp.round(quarters)
    t = (quarters - whole) * (math.pi / 2)
    s = t * t
    sin = t + t * s * (-1.6666654611e-1 + s * (8.3321608736e-3 - s * 1.9515295891e-4))
    cos = 1.0 - 0.5 * s + s * s * (4.166664568298827e-2 + s * (-1.388731625493765e-3 + s * 2.443315711809948e-5))
    n = whole.astype(jnp.int32)
    odd = (n & 1) == 1
    a = jnp.where(odd, sin, cos)
    b = jnp.where(odd, cos, sin)
    a = jnp.where(((n + 1) & 2) == 2, -a, a)
    b = jnp.where((n & 2) == 2, -b, b)
    return a, b

def wrapped(pixel):
    return (((pixel + N // 2) & (N - 1)) - N // 2).astype(F32) * (WIDTH / N)

def kernel(
    values_hbm, cell_hbm, offset_hbm, tile_hbm, band_hbm, depth_hbm,
    outer_hbm, twist_hbm, bands_hbm, turn_hbm, final_hbm, out,
    values, cell, offset, tile, band, depth_ref, outer, twist, bands, turn, final,
    vis_send, vis_recv, parts, tiles, spec, spill, col_send, col_recv, partial, screen, red_send, red_recv, lines, pairs, ready,
    load_sem, vis_ssem, vis_rsem, spill_ssem, spill_rsem, col_ssem, col_rsem, red_ssem, red_rsem,
):
    g, w = lax.axis_index("layer"), lax.axis_index("uvrow")
    z, x = w >> 2, w & 3

    barrier = pltpu.get_barrier_semaphore()
    loads = [
        pltpu.make_async_copy(there, here, load_sem.at[n])
        for n, (there, here) in enumerate(
            [
                (band_hbm, band), (tile_hbm, tile), (cell_hbm, cell), (offset_hbm, offset),
                (values_hbm, values), (depth_hbm, depth_ref), (twist_hbm, twist), (outer_hbm, outer),
                (bands_hbm, bands), (turn_hbm, turn), (final_hbm, final),
            ]
        )
    ]
    for load in loads:
        load.start()

    tier = tier_of(w)

    @pl.loop(0, BANDS - 1)
    def _(n):
        there = (w + far_first(n, BANDS)) & (BANDS - 1)

        @pl.when(tier_of(there) >= tier)
        def _():
            pl.semaphore_signal(barrier, inc=1, device_id={"layer": g, "uvrow": there}, device_id_type=MESH)

    @pl.loop(1, LAYERS)
    def _(i):
        pl.semaphore_signal(barrier, inc=1, device_id={"layer": g ^ i, "uvrow": w}, device_id_type=MESH)

    for load in loads[:6]:
        load.wait()

    row_id = lax.broadcasted_iota(jnp.int32, (BLOCKS, BLOCKS), 0)
    col_id = lax.broadcasted_iota(jnp.int32, (BLOCKS, BLOCKS), 1)
    other = jnp.broadcast_to(band[...], (BLOCKS, BLOCKS))
    own = jnp.sum(jnp.where(row_id == col_id, other, 0), axis=1, keepdims=True)
    tile_of = jnp.sum(jnp.where(row_id == col_id, jnp.broadcast_to(tile[...], (BLOCKS, BLOCKS)), 0), axis=1, keepdims=True)
    same = own == other
    rank = jnp.sum(jnp.where(same & (row_id < col_id), 1, 0), axis=0, keepdims=True)
    cells = cell[...].astype(F32)
    rows = jnp.floor((cells + 0.5) * (1.0 / SPAN))
    cols = cells - rows * SPAN
    shifts = offset[...]
    u_place = rows * 8.0 + (shifts >> 3).astype(F32)
    v_place = (cols + tile_of.astype(F32) * TW) * 8.0 + (shifts & 7).astype(F32)
    data = jnp.concatenate([values[:, 0, :], values[:, 1, :], u_place, v_place], axis=1)
    first = data.astype(BF16)
    rest = data - first.astype(F32)
    second = rest.astype(BF16)
    third = (rest - second.astype(F32)).astype(BF16)
    stacked = jnp.concatenate([first, second, third], axis=0)
    for j in range(2):
        pick = jnp.where((row_id == other) & (rank == j), 1.0, 0.0).astype(BF16)
        pick = jnp.concatenate([pick, pick, pick], axis=1)
        slots = lax.dot_general(pick, stacked, NN, preferred_element_type=F32)
        for f in range(4):
            vis_send[pl.ds(4 * j + f, BANDS, stride=8), :] = slots[:, f * 128 : (f + 1) * 128]

    depth = depth_ref[g]
    lane = lax.broadcasted_iota(jnp.int32, (64, 128), 1)
    y = wrapped((lane & 31) * 64 + lax.broadcasted_iota(jnp.int32, (64, 128), 0))

    @pl.loop(0, LAYERS)
    def _(k):
        xp = wrapped(256 * k + 4 * w + (lane >> 5))
        r = xp * xp + y * y
        turns = depth * (-r / (1.0 + jnp.sqrt(1.0 - r)))
        cos, sin = cos_sin_turns(turns)
        screen[k, 0] = cos * (1.0 / N)
        screen[k, 1] = sin * (1.0 / N)

    pl.semaphore_wait(barrier, BANDS - 2 * LATE - 1 + LATE * tier + LAYERS - 1)

    @pl.when(tier > 0)
    def _():
        @pl.loop(0, BANDS - 1)
        def _(n):
            there = (w + far_first(n, BANDS)) & (BANDS - 1)

            @pl.when(tier_of(there) < tier)
            def _():
                pl.semaphore_signal(
                    ready.at[tier - 1], inc=1, device_id={"layer": g, "uvrow": there}, device_id_type=MESH
                )

    def vis_copy(there):
        return pltpu.make_async_remote_copy(
            src_ref=vis_send.at[pl.ds(pl.multiple_of(there * 8, 8), 8)],
            dst_ref=vis_recv.at[pl.ds(pl.multiple_of(w * 8, 8), 8)],
            send_sem=vis_ssem,
            recv_sem=vis_rsem.at[w],
            device_id={"layer": g, "uvrow": there},
            device_id_type=MESH,
        )

    @pl.loop(0, BANDS - 1)
    def _(n):
        there = (w + far_first(n, BANDS)) & (BANDS - 1)

        @pl.when(tier_of(there) <= tier)
        def _():
            vis_copy(there).start()

    for later in range(2):

        @pl.when(tier <= later)
        def _():
            pl.semaphore_wait(ready.at[later], LATE)

            @pl.loop(0, LATE)
            def _(n):
                vis_copy(4 * (LATE * later + ((n + z) & (LATE - 1)))).start()

    mine = pl.ds(pl.multiple_of(w * 8, 8), 8)
    pltpu.make_async_copy(vis_send.at[mine], vis_recv.at[mine], vis_rsem.at[w]).start()
    for load in loads[6:]:
        load.wait()

    sublane = lax.broadcasted_iota(jnp.int32, (8, 128), 0)

    def source(n):
        block = n >> 4
        early = 4 * ((z + n) & 15) + 1 + lax.rem(x + block, 3)
        late = 4 * ((n & 8) + ((z + n) & 7))
        return jnp.where(block == 3, late, early)

    def taps(place):
        cell = place >> 3
        tap = (sublane - cell) & 7
        group = (cell + tap - sublane) >> 3
        far = (tap.astype(F32) - ((place & 7).astype(F32) * (1.0 / OVS) + (K - 1) / 2.0)) * TAP_SCALE
        return group, jnp.exp2(-(far * far))

    def spread(group, value, count):
        return jnp.concatenate([jnp.where(group == m, value, 0.0) for m in range(count)], axis=0)

    def split(value):
        high = value.astype(BF16).astype(F32)
        return high, value - high

    def patches(i, count):
        begins = [pl.multiple_of(source(i + n) * 8, 8) for n in range(count)]
        for n in range(count):
            piece = vis_recv.at[pl.ds(begins[n], 8)]
            pltpu.make_async_copy(piece, piece, vis_rsem.at[source(i + n)]).wait()
        for n in range(count):
            message = vis_recv[pl.ds(begins[n], 8), :]
            rows_high, rows_low, cols_high, cols_low = [], [], [], []
            for j in range(2):
                slot = (2 * (i + n) + j) & (SLOTS - 1)
                u_place = message[4 * j + 2 : 4 * j + 3].astype(jnp.int32)
                v_place = message[4 * j + 3 : 4 * j + 4].astype(jnp.int32)
                row_group, row_taps = taps(u_place)
                col_group, col_taps = taps(v_place & (TW * OVS - 1))
                re = split(row_taps * message[4 * j : 4 * j + 1])
                im = split(row_taps * message[4 * j + 1 : 4 * j + 2])
                cols = split(col_taps)
                wh, wl = [
                    jnp.concatenate(
                        [spread(row_group, re[p], EXT // 8), spread(row_group, im[p], EXT // 8)], axis=0
                    ).astype(BF16)
                    for p in range(2)
                ]
                ch, cl = [spread(col_group, cols[p], TW // 8).astype(BF16) for p in range(2)]
                rows_high.append(wh)
                rows_low.append(wl)
                cols_high.append(ch)
                cols_low.append(cl)
                number = (v_place >> 10).astype(F32)
                for copy in range(3):
                    tiles[pl.ds(copy * SLOTS + slot, 1), :] = number
            none = jnp.zeros((2 * EXT, 128), BF16)
            first = [jnp.concatenate([rows_high[0], none], axis=1), jnp.concatenate([none, rows_high[1]], axis=1)]
            low = lax.dot_general(
                jnp.concatenate(first, axis=0), jnp.concatenate(cols_low, axis=1), NT, preferred_element_type=F32
            )
            high = [lax.dot_general(jnp.concatenate([rows_high[j], rows_low[j]], axis=1), jnp.concatenate([cols_high[j], cols_high[j]], axis=1), NT, preferred_element_type=F32) for j in range(2)]
            patch = jnp.concatenate(high, axis=0) + low
            parts[pl.ds(pl.multiple_of(((2 * (i + n)) & (SLOTS - 1)) * 2 * EXT, 16), 4 * EXT), :] = patch

    p0 = lax.broadcasted_iota(jnp.int32, (16, 3 * SLOTS), 0).astype(F32)
    exact = lax.broadcasted_iota(jnp.int32, (32, 3 * SLOTS), 1) < 2 * SLOTS

    def tile_row(u, mix, begin):
        re = parts[pl.ds(u, SLOTS, stride=2 * EXT), :]
        im = parts[pl.ds(u + EXT, SLOTS, stride=2 * EXT), :]
        ph, plo = halves(jnp.concatenate([re, im], axis=1))
        both = lax.dot_general(
            mix, jnp.concatenate([ph, plo, ph], axis=0), NN, preferred_element_type=F32
        )
        re = both[:16, :128] - both[16:, 128:]
        im = both[:16, 128:] + both[16:, :128]
        tc, ts = twist[0], twist[1]
        at = pl.ds(pl.multiple_of(u * 16, 16), 16)
        new_re, new_im = re * tc - im * ts, re * ts + im * tc
        if begin:
            spec[0, at, :] = new_re
            spec[1, at, :] = new_im
        else:
            spec[0, at, :] += new_re
            spec[1, at, :] += new_im

    after = (w + 1) & (BANDS - 1)
    spill_copy = pltpu.make_async_remote_copy(
        src_ref=spec.at[:, pl.ds(ROWS * 16, (EXT - ROWS) * 16)],
        dst_ref=spill,
        send_sem=spill_ssem,
        recv_sem=spill_rsem,
        device_id={"layer": g, "uvrow": after},
        device_id_type=MESH,
    )
    for chunk in range(CHUNKS):
        start = chunk * (SLOTS // 2)

        @pl.loop(start, start + SLOTS // 2, step=GROUP)
        def _(i):
            patches(i, GROUP)

        by_slot = jnp.transpose(tiles[...])[:16, : 3 * SLOTS]
        cos, sin = cos_sin_turns(by_slot * p0 * (1.0 / 16))
        mh, ml = halves(jnp.concatenate([cos, sin], axis=0))
        mix = jnp.where(exact, mh, ml)

        @pl.loop(ROWS, EXT, step=ROW_GROUP)
        def _(u):
            for n in range(ROW_GROUP):
                tile_row(u + n, mix, chunk == 0)

        if chunk == CHUNKS - 1:
            spill_copy.start()

        @pl.loop(0, ROWS, step=ROW_GROUP)
        def _(u):
            for n in range(ROW_GROUP):
                tile_row(u + n, mix, chunk == 0)

    spill_copy.wait()
    over = pl.ds(0, (EXT - ROWS) * 16)
    spec[:, over, :] = spec[:, over, :] + spill[...]

    for ih in range(2):
        for dx in range(4):
            there_x = x ^ dx
            operand = []
            for il in range(2):
                place = pl.ds(4 * there_x + 2 * ih + il, ROWS, stride=16)
                re, im = spec[0, place, :], spec[1, place, :]
                operand.append(jnp.concatenate([re, -im], axis=1))
                operand.append(jnp.concatenate([im, re], axis=1))
            oh, ol = halves(jnp.concatenate(operand, axis=0))
            half = lax.dot_general(
                outer[...], jnp.concatenate([oh, ol, oh], axis=1), NT, preferred_element_type=F32
            )
            for there_z in range(16):
                at = pl.multiple_of((4 * there_z + there_x) * 8, 8)
                col_send[ih, pl.ds(at, 8), :] = half[8 * there_z : 8 * there_z + 8]

            @pl.loop(0, 16 if dx else 15)
            def _(n):
                there = (((z + far_first(n, 16)) & 15) << 2) + there_x
                pltpu.make_async_remote_copy(
                    src_ref=col_send.at[ih, pl.ds(pl.multiple_of(there * 8, 8), 8)],
                    dst_ref=col_recv.at[ih, pl.ds(pl.multiple_of(w * 8, 8), 8)],
                    send_sem=col_ssem,
                    recv_sem=col_rsem.at[ih],
                    device_id={"layer": g, "uvrow": there},
                    device_id_type=MESH,
                ).start()

    mine = pl.ds(pl.multiple_of(w * 8, 8), 8)
    for ih in range(2):
        col_recv[ih, mine, :] = col_send[ih, mine, :]

    def arrived(ih):
        others = col_recv.at[ih, pl.ds(0, (BANDS - 1) * 8)]
        pltpu.make_async_copy(others, others, col_rsem.at[ih]).wait()

    def half_image(ih, first, count):
        held = jnp.concatenate(
            [col_recv[ih, pl.ds(first + k, 64, stride=8), :] for k in range(count)], axis=1
        )
        hh, hl = halves(held)
        both = lax.dot_general(
            bands[...], jnp.concatenate([hh, hl, hh], axis=0), NN, preferred_element_type=F32
        )
        turned = []
        for k in range(count):
            a, b = both[:64, 128 * k : 128 * k + 128], both[64:, 128 * k : 128 * k + 128]
            turned.append(
                jnp.concatenate([a * turn[0] - b * turn[1], a * turn[1] + b * turn[0]], axis=1)
            )
        th, tl = halves(jnp.concatenate(turned, axis=0))
        return lax.dot_general(
            jnp.concatenate([th, tl, th], axis=1), final[ih], NN, preferred_element_type=F32
        )

    arrived(0)
    for first in range(0, LAYERS, 4):
        partial[64 * first : 64 * first + 256, :] = half_image(0, first, 4)

    def red_copy(there):
        return pltpu.make_async_remote_copy(
            src_ref=red_send.at[there],
            dst_ref=red_recv.at[g],
            send_sem=red_ssem,
            recv_sem=red_rsem,
            device_id={"layer": there, "uvrow": w},
            device_id_type=MESH,
        )

    arrived(1)
    for step in range(2):
        first = ((g >> 2) ^ (1 - step)) * 4
        image = half_image(1, first, 4) + partial[pl.ds(pl.multiple_of(first * 64, 256), 256), :]
        for n in range(4):
            there = first + n
            piece = image[64 * n : 64 * n + 64]
            red_send[there] = piece[:, :128] * screen[there, 0] - piece[:, 128:] * screen[there, 1]

            @pl.when(there != g)
            def _():
                red_copy(there).start()

    red_recv[g] = red_send[g]
    others = red_recv.at[pl.ds(0, LAYERS - 1)]
    pltpu.make_async_copy(others, others, red_rsem).wait()
    total = red_recv[0]
    for layer in range(1, LAYERS):
        total = total + red_recv[layer]
    lines[...] = jnp.transpose(total)
    pairs[...] = jnp.concatenate([lines[pl.ds(n, 64, stride=2), :] for n in range(2)], axis=1)
    for n in range(16):
        out[:, 128 * n : 128 * n + 128] = pairs[pl.ds(n, 4, stride=16), :]

    sent = vis_send.at[pl.ds(0, (BANDS - 1) * 8)]
    pltpu.make_async_copy(sent, sent, vis_ssem).wait()
    sent = col_send.at[:, pl.ds(0, (BANDS - 1) * 8)]
    pltpu.make_async_copy(sent, sent, col_ssem).wait()
    sent = red_send.at[pl.ds(0, LAYERS - 1)]
    pltpu.make_async_copy(sent, sent, red_ssem).wait()

def per_device(vis_values, vis_cell, vis_offset, block_tile, block_band, layer_w):
    tables = [jnp.asarray(t) for t in host_tables()]
    operands = [
        vis_values, vis_cell, vis_offset, block_tile.reshape(1, BLOCKS), block_band.reshape(1, BLOCKS), layer_w, *tables,
    ]
    hbm = pl.BlockSpec(memory_space=pltpu.HBM)
    vmem = pl.BlockSpec(memory_space=pltpu.VMEM)
    dma = pltpu.SemaphoreType.DMA
    held = [(pltpu.SMEM if a is layer_w else pltpu.VMEM)(a.shape, a.dtype) for a in operands]
    return pl.pallas_call(
        kernel,
        out_shape=jax.ShapeDtypeStruct((4, N), F32),
        in_specs=[hbm] * len(operands),
        out_specs=vmem,
        scratch_shapes=[
            *held,
            pltpu.VMEM((BANDS * 8, 128), F32),
            pltpu.VMEM((BANDS * 8, 128), F32),
            pltpu.VMEM((SLOTS * 2 * EXT, 128), F32),
            pltpu.VMEM((max(128, 3 * SLOTS), 128), F32),
            pltpu.VMEM((2, EXT * 16, 128), F32),
            pltpu.VMEM((2, (EXT - ROWS) * 16, 128), F32),
            pltpu.VMEM((2, BANDS * 8, 128), F32),
            pltpu.VMEM((2, BANDS * 8, 128), F32),
            pltpu.VMEM((LAYERS * 64, 256), F32),
            pltpu.VMEM((LAYERS, 2, 64, 128), F32),
            pltpu.VMEM((LAYERS, 64, 128), F32),
            pltpu.VMEM((LAYERS, 64, 128), F32),
            pltpu.VMEM((128, 64), F32),
            pltpu.VMEM((64, 128), F32),
            pltpu.SemaphoreType.REGULAR((2,)),
            dma((len(operands),)), dma, dma((BANDS,)), dma, dma, dma, dma((2,)), dma, dma,
        ],
        compiler_params=pltpu.CompilerParams(
            collective_id=0, has_side_effects=True, vmem_limit_bytes=60 * 1024 * 1024
        ),
    )(*operands)

def solution(mesh):
    placed = (
        P(("layer", "uvrow"), None, None),
        P(("layer", "uvrow"), None),
        P(("layer", "uvrow"), None),
        P(("layer", "uvrow"), None),
        P(("layer", "uvrow"), None),
        P(),
    )
    return jax.shard_map(
        per_device,
        mesh=mesh,
        in_specs=placed,
        out_specs=P(("layer", "uvrow"), None),
        check_vma=False,
    )
```

```python
import functools
import math

import jax
import jax.numpy as jnp
import ml_dtypes
import numpy as np
from jax import lax
from jax.experimental import pallas as pl
from jax.experimental.pallas import tpu as pltpu
from jax.sharding import PartitionSpec as P

N = 2048
TW = 128
K = 8
OVS = 8
SPAN = TW - K + 1
BANDS = 64
LAYERS = 8
BLOCKS = 64
ROWS = 32
EXT = 40
SIGMA = 1.45
WIDTH = 0.6
CHUNKS = 2
SLOTS = 2 * BANDS // CHUNKS
GROUP = 8
ROW_GROUP = 8
HALF = ROWS // 2
TAP_SCALE = math.sqrt(math.log2(math.e) / (2.0 * SIGMA * SIGMA))
MESH = pl.DeviceIdType.MESH
F32 = jnp.float32
BF16 = jnp.bfloat16
NN = (((1,), (0,)), ((), ()))
NT = (((1,), (1,)), ((), ()))

def far_first(n, count):
    return count // 2 + ((n + 1) >> 1) * (1 - 2 * (n & 1))

def near_first(n):
    return ((n + 2) >> 1) * (1 - 2 * (n & 1))

def halves(x):
    high = x.astype(BF16)
    low = (x - high.astype(F32)).astype(BF16)
    return high, low

def host_halves(x):
    high = x.astype(np.float32).astype(ml_dtypes.bfloat16)
    low = (x - high.astype(np.float64)).astype(np.float32).astype(ml_dtypes.bfloat16)
    return high, low

def host_tables():
    p1 = np.array([16 * k + z for z in range(16) for k in range(8)])
    col = np.arange(TW)
    angle = 2 * np.pi * ((p1[:, None] * col[None, :]) % TW) / TW
    high, low = host_halves(np.concatenate([np.cos(angle), np.sin(angle)], axis=1))
    outer = np.concatenate([high, high, low], axis=1)
    angle = 2 * np.pi * (np.arange(16)[:, None] * col[None, :]) / N
    twist = np.stack([np.cos(angle), np.sin(angle)]).astype(np.float32)
    q0 = np.arange(64)
    angle = 2 * np.pi * ((q0[:, None] * q0[None, :]) % 64) / 64
    high, low = host_halves(np.concatenate([np.cos(angle), np.sin(angle)], axis=0))
    bands = np.concatenate([high, high, low], axis=1)
    r = np.arange(ROWS)
    angle = 2 * np.pi * (q0[:, None] * r[None, :]) / N
    cos, sin = np.cos(angle), np.sin(angle)
    spans = [slice(HALF, ROWS), slice(0, HALF)]
    turn = np.stack(
        [
            np.concatenate([a[:, span], b[:, span]] * 4, axis=1)
            for span in spans
            for a, b in ((cos, -sin), (sin, cos))
        ]
    ).astype(np.float32)
    angle = 2 * np.pi * ((r[:, None] * r[None, :]) % ROWS) / ROWS
    cos, sin = np.cos(angle), np.sin(angle)
    last = np.zeros((2, 2, 4, 2, HALF, 2, 4, ROWS))
    for half in range(2):
        for i in range(4):
            for c in range(2):
                last[half, 0, i, c, :, 0, i, :] = cos[spans[half]]
                last[half, 0, i, c, :, 1, i, :] = sin[spans[half]]
                last[half, 1, i, c, :, 0, i, :] = -sin[spans[half]]
                last[half, 1, i, c, :, 1, i, :] = cos[spans[half]]
    high, low = host_halves(last.reshape(2, 256, 256))
    final = np.concatenate([high, high, low], axis=1)
    return outer, twist, bands, turn, final

def cos_sin_turns(turns):
    quarters = turns * 4.0
    whole = jnp.round(quarters)
    t = (quarters - whole) * (math.pi / 2)
    s = t * t
    sin = t + t * s * (-1.6666654611e-1 + s * (8.3321608736e-3 - s * 1.9515295891e-4))
    cos = 1.0 - 0.5 * s + s * s * (4.166664568298827e-2 + s * (-1.388731625493765e-3 + s * 2.443315711809948e-5))
    n = whole.astype(jnp.int32)
    odd = (n & 1) == 1
    a = jnp.where(odd, sin, cos)
    b = jnp.where(odd, cos, sin)
    a = jnp.where(((n + 1) & 2) == 2, -a, a)
    b = jnp.where((n & 2) == 2, -b, b)
    return a, b

def wrapped(pixel):
    return (((pixel + N // 2) & (N - 1)) - N // 2).astype(F32) * (WIDTH / N)

def kernel(
    values_hbm, cell_hbm, offset_hbm, tile_hbm, band_hbm, depth_hbm,
    outer_hbm, twist_hbm, bands_hbm, turn_hbm, final_hbm, out,
    values, cell, offset, tile, band, depth_ref, outer, twist, bands, turn, final,
    vis_send, vis_recv, parts, tiles, spec, spill, col_send, col_recv, partial, screen, red_send, red_recv, lines, pairs,
    load_sem, vis_ssem, vis_rsem, spill_ssem, spill_rsem, col_ssem, col_rsem, red_ssem, red_rsem,
):
    g, w = lax.axis_index("layer"), lax.axis_index("uvrow")
    z, x = w >> 2, w & 3

    barrier = pltpu.get_barrier_semaphore()
    loads = [
        pltpu.make_async_copy(there, here, load_sem.at[n])
        for n, (there, here) in enumerate(
            [
                (band_hbm, band), (tile_hbm, tile), (cell_hbm, cell), (offset_hbm, offset),
                (values_hbm, values), (depth_hbm, depth_ref), (twist_hbm, twist), (outer_hbm, outer),
                (bands_hbm, bands), (turn_hbm, turn), (final_hbm, final),
            ]
        )
    ]
    for load in loads:
        load.start()

    @pl.loop(0, BANDS - 1)
    def _(n):
        there = (w + far_first(n, BANDS)) & (BANDS - 1)
        pl.semaphore_signal(barrier, inc=1, device_id={"layer": g, "uvrow": there}, device_id_type=MESH)

    @pl.loop(1, LAYERS)
    def _(i):
        pl.semaphore_signal(barrier, inc=1, device_id={"layer": g ^ i, "uvrow": w}, device_id_type=MESH)

    for load in loads[:6]:
        load.wait()

    row_id = lax.broadcasted_iota(jnp.int32, (BLOCKS, BLOCKS), 0)
    col_id = lax.broadcasted_iota(jnp.int32, (BLOCKS, BLOCKS), 1)
    other = jnp.broadcast_to(band[...], (BLOCKS, BLOCKS))
    own = jnp.sum(jnp.where(row_id == col_id, other, 0), axis=1, keepdims=True)
    tile_of = jnp.sum(jnp.where(row_id == col_id, jnp.broadcast_to(tile[...], (BLOCKS, BLOCKS)), 0), axis=1, keepdims=True)
    same = own == other
    rank = jnp.sum(jnp.where(same & (row_id < col_id), 1, 0), axis=0, keepdims=True)
    cells = cell[...].astype(F32)
    rows = jnp.floor((cells + 0.5) * (1.0 / SPAN))
    cols = cells - rows * SPAN
    shifts = offset[...]
    u_place = rows * 8.0 + (shifts >> 3).astype(F32)
    v_place = (cols + tile_of.astype(F32) * TW) * 8.0 + (shifts & 7).astype(F32)
    data = jnp.concatenate([values[:, 0, :], values[:, 1, :], u_place, v_place], axis=1)
    first = data.astype(BF16)
    rest = data - first.astype(F32)
    second = rest.astype(BF16)
    third = (rest - second.astype(F32)).astype(BF16)
    stacked = jnp.concatenate([first, second, third], axis=0)
    for j in range(2):
        pick = jnp.where((row_id == other) & (rank == j), 1.0, 0.0).astype(BF16)
        pick = jnp.concatenate([pick, pick, pick], axis=1)
        slots = lax.dot_general(pick, stacked, NN, preferred_element_type=F32)
        for f in range(4):
            vis_send[pl.ds(4 * j + f, BANDS, stride=8), :] = slots[:, f * 128 : (f + 1) * 128]

    depth = depth_ref[g]
    lane = lax.broadcasted_iota(jnp.int32, (64, 128), 1)
    y = wrapped((lane & 31) * 64 + lax.broadcasted_iota(jnp.int32, (64, 128), 0))

    @pl.loop(0, LAYERS)
    def _(k):
        xp = wrapped(256 * k + 4 * w + (lane >> 5))
        r = xp * xp + y * y
        turns = depth * (-r / (1.0 + jnp.sqrt(1.0 - r)))
        cos, sin = cos_sin_turns(turns)
        screen[k, 0] = cos * (1.0 / N)
        screen[k, 1] = sin * (1.0 / N)

    pl.semaphore_wait(barrier, BANDS - 1 + LAYERS - 1)

    def vis_copy(there):
        return pltpu.make_async_remote_copy(
            src_ref=vis_send.at[pl.ds(pl.multiple_of(there * 8, 8), 8)],
            dst_ref=vis_recv.at[pl.ds(pl.multiple_of(w * 8, 8), 8)],
            send_sem=vis_ssem,
            recv_sem=vis_rsem.at[w],
            device_id={"layer": g, "uvrow": there},
            device_id_type=MESH,
        )

    @pl.loop(0, BANDS - 1)
    def _(n):
        vis_copy((w + near_first(n)) & (BANDS - 1)).start()

    mine = pl.ds(pl.multiple_of(w * 8, 8), 8)
    pltpu.make_async_copy(vis_send.at[mine], vis_recv.at[mine], vis_rsem.at[w]).start()
    for load in loads[6:]:
        load.wait()

    sublane = lax.broadcasted_iota(jnp.int32, (8, 128), 0)

    def source(n):
        return jnp.where(n == 0, w, (w - near_first(n - 1)) & (BANDS - 1))

    def taps(place):
        cell = place >> 3
        tap = (sublane - cell) & 7
        group = (cell + tap - sublane) >> 3
        far = (tap.astype(F32) - ((place & 7).astype(F32) * (1.0 / OVS) + (K - 1) / 2.0)) * TAP_SCALE
        return group, jnp.exp2(-(far * far))

    def spread(group, value, count):
        return jnp.concatenate([jnp.where(group == m, value, 0.0) for m in range(count)], axis=0)

    def split(value):
        high = value.astype(BF16).astype(F32)
        return high, value - high

    def patches(i, count):
        begins = [pl.multiple_of(source(i + n) * 8, 8) for n in range(count)]
        for n in range(count):
            piece = vis_recv.at[pl.ds(begins[n], 8)]
            pltpu.make_async_copy(piece, piece, vis_rsem.at[source(i + n)]).wait()
        for n in range(count):
            message = vis_recv[pl.ds(begins[n], 8), :]
            rows_high, rows_low, cols_high, cols_low = [], [], [], []
            for j in range(2):
                slot = (2 * (i + n) + j) & (SLOTS - 1)
                u_place = message[4 * j + 2 : 4 * j + 3].astype(jnp.int32)
                v_place = message[4 * j + 3 : 4 * j + 4].astype(jnp.int32)
                row_group, row_taps = taps(u_place)
                col_group, col_taps = taps(v_place & (TW * OVS - 1))
                re = split(row_taps * message[4 * j : 4 * j + 1])
                im = split(row_taps * message[4 * j + 1 : 4 * j + 2])
                cols = split(col_taps)
                wh, wl = [
                    jnp.concatenate(
                        [spread(row_group, re[p], EXT // 8), spread(row_group, im[p], EXT // 8)], axis=0
                    ).astype(BF16)
                    for p in range(2)
                ]
                ch, cl = [spread(col_group, cols[p], TW // 8).astype(BF16) for p in range(2)]
                rows_high.append(wh)
                rows_low.append(wl)
                cols_high.append(ch)
                cols_low.append(cl)
                number = (v_place >> 10).astype(F32)
                for copy in range(3):
                    tiles[pl.ds(copy * SLOTS + slot, 1), :] = number
            none = jnp.zeros((2 * EXT, 128), BF16)
            first = [jnp.concatenate([rows_high[0], none], axis=1), jnp.concatenate([none, rows_high[1]], axis=1)]
            low = lax.dot_general(
                jnp.concatenate(first, axis=0), jnp.concatenate(cols_low, axis=1), NT, preferred_element_type=F32
            )
            high = [lax.dot_general(jnp.concatenate([rows_high[j], rows_low[j]], axis=1), jnp.concatenate([cols_high[j], cols_high[j]], axis=1), NT, preferred_element_type=F32) for j in range(2)]
            patch = jnp.concatenate(high, axis=0) + low
            parts[pl.ds(pl.multiple_of(((2 * (i + n)) & (SLOTS - 1)) * 2 * EXT, 16), 4 * EXT), :] = patch

    p0 = lax.broadcasted_iota(jnp.int32, (16, 3 * SLOTS), 0).astype(F32)
    exact = lax.broadcasted_iota(jnp.int32, (32, 3 * SLOTS), 1) < 2 * SLOTS

    def tile_row(u, mix, begin):
        re = parts[pl.ds(u, SLOTS, stride=2 * EXT), :]
        im = parts[pl.ds(u + EXT, SLOTS, stride=2 * EXT), :]
        ph, plo = halves(jnp.concatenate([re, im], axis=1))
        both = lax.dot_general(
            mix, jnp.concatenate([ph, plo, ph], axis=0), NN, preferred_element_type=F32
        )
        re = both[:16, :128] - both[16:, 128:]
        im = both[:16, 128:] + both[16:, :128]
        tc, ts = twist[0], twist[1]
        at = pl.ds(pl.multiple_of(u * 16, 16), 16)
        new_re, new_im = re * tc - im * ts, re * ts + im * tc
        if begin:
            spec[0, at, :] = new_re
            spec[1, at, :] = new_im
        else:
            spec[0, at, :] += new_re
            spec[1, at, :] += new_im

    after = (w + 1) & (BANDS - 1)
    spill_copy = pltpu.make_async_remote_copy(
        src_ref=spec.at[:, pl.ds(ROWS * 16, (EXT - ROWS) * 16)],
        dst_ref=spill,
        send_sem=spill_ssem,
        recv_sem=spill_rsem,
        device_id={"layer": g, "uvrow": after},
        device_id_type=MESH,
    )
    for chunk in range(CHUNKS):
        start = chunk * (SLOTS // 2)

        @pl.loop(start, start + SLOTS // 2, step=GROUP)
        def _(i):
            patches(i, GROUP)

        by_slot = jnp.transpose(tiles[...])[:16, : 3 * SLOTS]
        cos, sin = cos_sin_turns(by_slot * p0 * (1.0 / 16))
        mh, ml = halves(jnp.concatenate([cos, sin], axis=0))
        mix = jnp.where(exact, mh, ml)

        def tile_rows(first, last):
            @pl.loop(first, last, step=ROW_GROUP)
            def _(u):
                for n in range(ROW_GROUP):
                    tile_row(u + n, mix, chunk == 0)

        tile_rows(ROWS, EXT)
        if chunk == CHUNKS - 1:
            spill_copy.start()
        else:
            tile_rows(0, ROWS)

    for half in range(2):
        begin = (1 - half) * HALF
        tile_rows(begin, begin + HALF)
        if half == 1:
            spill_copy.wait()
            over = pl.ds(0, (EXT - ROWS) * 16)
            spec[:, over, :] = spec[:, over, :] + spill[...]

        for dx in range(4):
            there_x = (x + dx) & 3
            operand = []
            for i in range(4):
                place = pl.ds(begin * 16 + 4 * there_x + i, HALF, stride=16)
                re, im = spec[0, place, :], spec[1, place, :]
                operand.append(jnp.concatenate([re, -im], axis=1))
                operand.append(jnp.concatenate([im, re], axis=1))
            oh, ol = halves(jnp.concatenate(operand, axis=0))
            rows = lax.dot_general(
                outer[...], jnp.concatenate([oh, ol, oh], axis=1), NT, preferred_element_type=F32
            )
            for there_z in range(16):
                at = pl.multiple_of((4 * there_z + there_x) * 8, 8)
                col_send[half, pl.ds(at, 8), :] = rows[8 * there_z : 8 * there_z + 8]

            @pl.loop(0, 16 if dx else 15)
            def _(n):
                there = (((z + far_first(n, 16)) & 15) << 2) + there_x
                pltpu.make_async_remote_copy(
                    src_ref=col_send.at[half, pl.ds(pl.multiple_of(there * 8, 8), 8)],
                    dst_ref=col_recv.at[half, pl.ds(pl.multiple_of(w * 8, 8), 8)],
                    send_sem=col_ssem,
                    recv_sem=col_rsem.at[half],
                    device_id={"layer": g, "uvrow": there},
                    device_id_type=MESH,
                ).start()

    mine = pl.ds(pl.multiple_of(w * 8, 8), 8)
    for half in range(2):
        col_recv[half, mine, :] = col_send[half, mine, :]

    def arrived(half):
        others = col_recv.at[half, pl.ds(0, (BANDS - 1) * 8)]
        pltpu.make_async_copy(others, others, col_rsem.at[half]).wait()

    def half_image(half, first, count):
        held = jnp.concatenate(
            [col_recv[half, pl.ds(first + k, 64, stride=8), :] for k in range(count)], axis=1
        )
        hh, hl = halves(held)
        both = lax.dot_general(
            bands[...], jnp.concatenate([hh, hl, hh], axis=0), NN, preferred_element_type=F32
        )
        turned = []
        for k in range(count):
            a, b = both[:64, 128 * k : 128 * k + 128], both[64:, 128 * k : 128 * k + 128]
            turned.append(
                jnp.concatenate([a * turn[2 * half] - b * turn[2 * half + 1], a * turn[2 * half + 1] + b * turn[2 * half]], axis=1)
            )
        th, tl = halves(jnp.concatenate(turned, axis=0))
        return lax.dot_general(
            jnp.concatenate([th, tl, th], axis=1), final[half], NN, preferred_element_type=F32
        )

    arrived(0)
    for first in range(0, LAYERS, 4):
        partial[64 * first : 64 * first + 256, :] = half_image(0, first, 4)

    def red_copy(there):
        return pltpu.make_async_remote_copy(
            src_ref=red_send.at[there],
            dst_ref=red_recv.at[g],
            send_sem=red_ssem,
            recv_sem=red_rsem,
            device_id={"layer": there, "uvrow": w},
            device_id_type=MESH,
        )

    arrived(1)
    for step in range(2):
        first = ((g >> 2) ^ (1 - step)) * 4
        image = half_image(1, first, 4) + partial[pl.ds(pl.multiple_of(first * 64, 256), 256), :]
        for n in range(4):
            there = first + n
            piece = image[64 * n : 64 * n + 64]
            red_send[there] = piece[:, :128] * screen[there, 0] - piece[:, 128:] * screen[there, 1]

            @pl.when(there != g)
            def _():
                red_copy(there).start()

    red_recv[g] = red_send[g]
    others = red_recv.at[pl.ds(0, LAYERS - 1)]
    pltpu.make_async_copy(others, others, red_rsem).wait()
    total = red_recv[0]
    for layer in range(1, LAYERS):
        total = total + red_recv[layer]
    lines[...] = jnp.transpose(total)
    pairs[...] = jnp.concatenate([lines[pl.ds(n, 64, stride=2), :] for n in range(2)], axis=1)
    for n in range(16):
        out[:, 128 * n : 128 * n + 128] = pairs[pl.ds(n, 4, stride=16), :]

    sent = vis_send.at[pl.ds(0, (BANDS - 1) * 8)]
    pltpu.make_async_copy(sent, sent, vis_ssem).wait()
    sent = col_send.at[:, pl.ds(0, (BANDS - 1) * 8)]
    pltpu.make_async_copy(sent, sent, col_ssem).wait()
    sent = red_send.at[pl.ds(0, LAYERS - 1)]
    pltpu.make_async_copy(sent, sent, red_ssem).wait()

def per_device(vis_values, vis_cell, vis_offset, block_tile, block_band, layer_w):
    tables = [jnp.asarray(t) for t in host_tables()]
    operands = [
        vis_values, vis_cell, vis_offset, block_tile.reshape(1, BLOCKS), block_band.reshape(1, BLOCKS), layer_w, *tables,
    ]
    hbm = pl.BlockSpec(memory_space=pltpu.HBM)
    vmem = pl.BlockSpec(memory_space=pltpu.VMEM)
    dma = pltpu.SemaphoreType.DMA
    held = [(pltpu.SMEM if a is layer_w else pltpu.VMEM)(a.shape, a.dtype) for a in operands]
    return pl.pallas_call(
        kernel,
        out_shape=jax.ShapeDtypeStruct((4, N), F32),
        in_specs=[hbm] * len(operands),
        out_specs=vmem,
        scratch_shapes=[
            *held,
            pltpu.VMEM((BANDS * 8, 128), F32),
            pltpu.VMEM((BANDS * 8, 128), F32),
            pltpu.VMEM((SLOTS * 2 * EXT, 128), F32),
            pltpu.VMEM((max(128, 3 * SLOTS), 128), F32),
            pltpu.VMEM((2, EXT * 16, 128), F32),
            pltpu.VMEM((2, (EXT - ROWS) * 16, 128), F32),
            pltpu.VMEM((2, BANDS * 8, 128), F32),
            pltpu.VMEM((2, BANDS * 8, 128), F32),
            pltpu.VMEM((LAYERS * 64, 256), F32),
            pltpu.VMEM((LAYERS, 2, 64, 128), F32),
            pltpu.VMEM((LAYERS, 64, 128), F32),
            pltpu.VMEM((LAYERS, 64, 128), F32),
            pltpu.VMEM((128, 64), F32),
            pltpu.VMEM((64, 128), F32),
            dma((len(operands),)), dma, dma((BANDS,)), dma, dma, dma, dma((2,)), dma, dma,
        ],
        compiler_params=pltpu.CompilerParams(
            collective_id=0, has_side_effects=True, vmem_limit_bytes=60 * 1024 * 1024
        ),
    )(*operands)

def solution(mesh):
    placed = (
        P(("layer", "uvrow"), None, None),
        P(("layer", "uvrow"), None),
        P(("layer", "uvrow"), None),
        P(("layer", "uvrow"), None),
        P(("layer", "uvrow"), None),
        P(),
    )
    return jax.shard_map(
        per_device,
        mesh=mesh,
        in_specs=placed,
        out_specs=P(("layer", "uvrow"), None),
        check_vma=False,
    )
```

```python
import functools
import math

import jax
import jax.numpy as jnp
import ml_dtypes
import numpy as np
from jax import lax
from jax.experimental import pallas as pl
from jax.experimental.pallas import tpu as pltpu
from jax.sharding import PartitionSpec as P

N = 2048
TW = 128
K = 8
OVS = 8
SPAN = TW - K + 1
BANDS = 64
LAYERS = 8
BLOCKS = 64
ROWS = 32
EXT = 40
SIGMA = 1.45
WIDTH = 0.6
CHUNKS = 2
SLOTS = 2 * BANDS // CHUNKS
GROUP = 4
ROW_GROUP = 8
HALF = ROWS // 2
TAP_SCALE = math.sqrt(math.log2(math.e) / (2.0 * SIGMA * SIGMA))
MESH = pl.DeviceIdType.MESH
F32 = jnp.float32
BF16 = jnp.bfloat16
NN = (((1,), (0,)), ((), ()))
NT = (((1,), (1,)), ((), ()))

def far_first(n, count):
    return count // 2 + ((n + 1) >> 1) * (1 - 2 * (n & 1))

def near_first(n):
    return ((n + 2) >> 1) * (1 - 2 * (n & 1))

def halves(x):
    high = x.astype(BF16)
    low = (x - high.astype(F32)).astype(BF16)
    return high, low

def host_halves(x):
    high = x.astype(np.float32).astype(ml_dtypes.bfloat16)
    low = (x - high.astype(np.float64)).astype(np.float32).astype(ml_dtypes.bfloat16)
    return high, low

def host_tables():
    p1 = np.array([16 * k + z for z in range(16) for k in range(8)])
    col = np.arange(TW)
    angle = 2 * np.pi * ((p1[:, None] * col[None, :]) % TW) / TW
    high, low = host_halves(np.concatenate([np.cos(angle), np.sin(angle)], axis=1))
    outer = np.concatenate([high, high, low], axis=1)
    angle = 2 * np.pi * (np.arange(16)[:, None] * col[None, :]) / N
    twist = np.stack([np.cos(angle), np.sin(angle)]).astype(np.float32)
    q0 = np.arange(64)
    angle = 2 * np.pi * ((q0[:, None] * q0[None, :]) % 64) / 64
    high, low = host_halves(np.concatenate([np.cos(angle), np.sin(angle)], axis=0))
    bands = np.concatenate([high, high, low], axis=1)
    r = np.arange(ROWS)
    angle = 2 * np.pi * (q0[:, None] * r[None, :]) / N
    cos, sin = np.cos(angle), np.sin(angle)
    spans = [slice(HALF, ROWS), slice(0, HALF)]
    turn = np.stack(
        [
            np.concatenate([a[:, span], b[:, span]] * 4, axis=1)
            for span in spans
            for a, b in ((cos, -sin), (sin, cos))
        ]
    ).astype(np.float32)
    angle = 2 * np.pi * ((r[:, None] * r[None, :]) % ROWS) / ROWS
    cos, sin = np.cos(angle), np.sin(angle)
    last = np.zeros((2, 2, 4, 2, HALF, 2, 4, ROWS))
    for half in range(2):
        for i in range(4):
            for c in range(2):
                last[half, 0, i, c, :, 0, i, :] = cos[spans[half]]
                last[half, 0, i, c, :, 1, i, :] = sin[spans[half]]
                last[half, 1, i, c, :, 0, i, :] = -sin[spans[half]]
                last[half, 1, i, c, :, 1, i, :] = cos[spans[half]]
    high, low = host_halves(last.reshape(2, 256, 256))
    final = np.concatenate([high, high, low], axis=1)
    return outer, twist, bands, turn, final

def cos_sin_turns(turns):
    quarters = turns * 4.0
    whole = jnp.round(quarters)
    t = (quarters - whole) * (math.pi / 2)
    s = t * t
    sin = t + t * s * (-1.6666654611e-1 + s * (8.3321608736e-3 - s * 1.9515295891e-4))
    cos = 1.0 - 0.5 * s + s * s * (4.166664568298827e-2 + s * (-1.388731625493765e-3 + s * 2.443315711809948e-5))
    n = whole.astype(jnp.int32)
    odd = (n & 1) == 1
    a = jnp.where(odd, sin, cos)
    b = jnp.where(odd, cos, sin)
    a = jnp.where(((n + 1) & 2) == 2, -a, a)
    b = jnp.where((n & 2) == 2, -b, b)
    return a, b

def wrapped(pixel):
    return (((pixel + N // 2) & (N - 1)) - N // 2).astype(F32) * (WIDTH / N)

def kernel(
    values_hbm, cell_hbm, offset_hbm, tile_hbm, band_hbm, depth_hbm,
    outer_hbm, twist_hbm, bands_hbm, turn_hbm, final_hbm, out,
    values, cell, offset, tile, band, depth_ref, outer, twist, bands, turn, final,
    vis_send, vis_recv, parts, tiles, spec, spill, col_send, col_recv, partial, screen, red_send, red_recv, lines, pairs,
    load_sem, vis_ssem, vis_rsem, spill_ssem, spill_rsem, col_ssem, col_rsem, red_ssem, red_rsem,
):
    g, w = lax.axis_index("layer"), lax.axis_index("uvrow")
    z, x = w >> 2, w & 3

    barrier = pltpu.get_barrier_semaphore()
    loads = [
        pltpu.make_async_copy(there, here, load_sem.at[n])
        for n, (there, here) in enumerate(
            [
                (band_hbm, band), (tile_hbm, tile), (cell_hbm, cell), (offset_hbm, offset),
                (values_hbm, values), (depth_hbm, depth_ref), (twist_hbm, twist), (outer_hbm, outer),
                (bands_hbm, bands), (turn_hbm, turn), (final_hbm, final),
            ]
        )
    ]
    for load in loads:
        load.start()

    @pl.loop(0, BANDS - 1)
    def _(n):
        there = (w + far_first(n, BANDS)) & (BANDS - 1)
        pl.semaphore_signal(barrier, inc=1, device_id={"layer": g, "uvrow": there}, device_id_type=MESH)

    @pl.loop(1, LAYERS)
    def _(i):
        pl.semaphore_signal(barrier, inc=1, device_id={"layer": g ^ i, "uvrow": w}, device_id_type=MESH)

    for load in loads[:6]:
        load.wait()

    row_id = lax.broadcasted_iota(jnp.int32, (BLOCKS, BLOCKS), 0)
    col_id = lax.broadcasted_iota(jnp.int32, (BLOCKS, BLOCKS), 1)
    other = jnp.broadcast_to(band[...], (BLOCKS, BLOCKS))
    own = jnp.sum(jnp.where(row_id == col_id, other, 0), axis=1, keepdims=True)
    tile_of = jnp.sum(jnp.where(row_id == col_id, jnp.broadcast_to(tile[...], (BLOCKS, BLOCKS)), 0), axis=1, keepdims=True)
    same = own == other
    rank = jnp.sum(jnp.where(same & (row_id < col_id), 1, 0), axis=0, keepdims=True)
    cells = cell[...].astype(F32)
    rows = jnp.floor((cells + 0.5) * (1.0 / SPAN))
    cols = cells - rows * SPAN
    shifts = offset[...]
    u_place = rows * 8.0 + (shifts >> 3).astype(F32)
    v_place = (cols + tile_of.astype(F32) * TW) * 8.0 + (shifts & 7).astype(F32)
    data = jnp.concatenate([values[:, 0, :], values[:, 1, :], u_place, v_place], axis=1)
    first = data.astype(BF16)
    rest = data - first.astype(F32)
    second = rest.astype(BF16)
    third = (rest - second.astype(F32)).astype(BF16)
    stacked = jnp.concatenate([first, second, third], axis=0)
    for j in range(2):
        pick = jnp.where((row_id == other) & (rank == j), 1.0, 0.0).astype(BF16)
        pick = jnp.concatenate([pick, pick, pick], axis=1)
        slots = lax.dot_general(pick, stacked, NN, preferred_element_type=F32)
        for f in range(4):
            vis_send[pl.ds(4 * j + f, BANDS, stride=8), :] = slots[:, f * 128 : (f + 1) * 128]

    depth = depth_ref[g]
    lane = lax.broadcasted_iota(jnp.int32, (64, 128), 1)
    y = wrapped((lane & 31) * 64 + lax.broadcasted_iota(jnp.int32, (64, 128), 0))

    @pl.loop(0, LAYERS)
    def _(k):
        xp = wrapped(256 * k + 4 * w + (lane >> 5))
        r = xp * xp + y * y
        turns = depth * (-r / (1.0 + jnp.sqrt(1.0 - r)))
        cos, sin = cos_sin_turns(turns)
        screen[k, 0] = cos * (1.0 / N)
        screen[k, 1] = sin * (1.0 / N)

    pl.semaphore_wait(barrier, BANDS - 1 + LAYERS - 1)

    def vis_copy(there):
        return pltpu.make_async_remote_copy(
            src_ref=vis_send.at[pl.ds(pl.multiple_of(there * 8, 8), 8)],
            dst_ref=vis_recv.at[pl.ds(pl.multiple_of(w * 8, 8), 8)],
            send_sem=vis_ssem,
            recv_sem=vis_rsem.at[w],
            device_id={"layer": g, "uvrow": there},
            device_id_type=MESH,
        )

    @pl.loop(0, BANDS - 1)
    def _(n):
        vis_copy((w + near_first(n)) & (BANDS - 1)).start()

    mine = pl.ds(pl.multiple_of(w * 8, 8), 8)
    pltpu.make_async_copy(vis_send.at[mine], vis_recv.at[mine], vis_rsem.at[w]).start()
    for load in loads[6:]:
        load.wait()

    sublane = lax.broadcasted_iota(jnp.int32, (8, 128), 0)

    def source(n):
        return jnp.where(n == 0, w, (w - near_first(n - 1)) & (BANDS - 1))

    def taps(place):
        cell = place >> 3
        tap = (sublane - cell) & 7
        group = (cell + tap - sublane) >> 3
        far = (tap.astype(F32) - ((place & 7).astype(F32) * (1.0 / OVS) + (K - 1) / 2.0)) * TAP_SCALE
        return group, jnp.exp2(-(far * far))

    def spread(group, value, count):
        return jnp.concatenate([jnp.where(group == m, value, 0.0) for m in range(count)], axis=0)

    def split(value):
        high = value.astype(BF16).astype(F32)
        return high, value - high

    def patches(i, count):
        begins = [pl.multiple_of(source(i + n) * 8, 8) for n in range(count)]
        for n in range(count):
            piece = vis_recv.at[pl.ds(begins[n], 8)]
            pltpu.make_async_copy(piece, piece, vis_rsem.at[source(i + n)]).wait()
        for n in range(count):
            message = vis_recv[pl.ds(begins[n], 8), :]
            rows_high, rows_low, cols_high, cols_low = [], [], [], []
            for j in range(2):
                slot = (2 * (i + n) + j) & (SLOTS - 1)
                u_place = message[4 * j + 2 : 4 * j + 3].astype(jnp.int32)
                v_place = message[4 * j + 3 : 4 * j + 4].astype(jnp.int32)
                row_group, row_taps = taps(u_place)
                col_group, col_taps = taps(v_place & (TW * OVS - 1))
                re = split(row_taps * message[4 * j : 4 * j + 1])
                im = split(row_taps * message[4 * j + 1 : 4 * j + 2])
                cols = split(col_taps)
                wh, wl = [
                    jnp.concatenate(
                        [spread(row_group, re[p], EXT // 8), spread(row_group, im[p], EXT // 8)], axis=0
                    ).astype(BF16)
                    for p in range(2)
                ]
                ch, cl = [spread(col_group, cols[p], TW // 8).astype(BF16) for p in range(2)]
                rows_high.append(wh)
                rows_low.append(wl)
                cols_high.append(ch)
                cols_low.append(cl)
                number = (v_place >> 10).astype(F32)
                for copy in range(3):
                    tiles[pl.ds(copy * SLOTS + slot, 1), :] = number
            none = jnp.zeros((2 * EXT, 128), BF16)
            first = [jnp.concatenate([rows_high[0], none], axis=1), jnp.concatenate([none, rows_high[1]], axis=1)]
            low = lax.dot_general(
                jnp.concatenate(first, axis=0), jnp.concatenate(cols_low, axis=1), NT, preferred_element_type=F32
            )
            high = [lax.dot_general(jnp.concatenate([rows_high[j], rows_low[j]], axis=1), jnp.concatenate([cols_high[j], cols_high[j]], axis=1), NT, preferred_element_type=F32) for j in range(2)]
            patch = jnp.concatenate(high, axis=0) + low
            parts[pl.ds(pl.multiple_of(((2 * (i + n)) & (SLOTS - 1)) * 2 * EXT, 16), 4 * EXT), :] = patch

    p0 = lax.broadcasted_iota(jnp.int32, (16, 3 * SLOTS), 0).astype(F32)
    exact = lax.broadcasted_iota(jnp.int32, (32, 3 * SLOTS), 1) < 2 * SLOTS

    def tile_row(u, mix, begin):
        re = parts[pl.ds(u, SLOTS, stride=2 * EXT), :]
        im = parts[pl.ds(u + EXT, SLOTS, stride=2 * EXT), :]
        ph, plo = halves(jnp.concatenate([re, im], axis=1))
        both = lax.dot_general(
            mix, jnp.concatenate([ph, plo, ph], axis=0), NN, preferred_element_type=F32
        )
        re = both[:16, :128] - both[16:, 128:]
        im = both[:16, 128:] + both[16:, :128]
        tc, ts = twist[0], twist[1]
        at = pl.ds(pl.multiple_of(u * 16, 16), 16)
        new_re, new_im = re * tc - im * ts, re * ts + im * tc
        if begin:
            spec[0, at, :] = new_re
            spec[1, at, :] = new_im
        else:
            spec[0, at, :] += new_re
            spec[1, at, :] += new_im

    after = (w + 1) & (BANDS - 1)
    spill_copy = pltpu.make_async_remote_copy(
        src_ref=spec.at[:, pl.ds(ROWS * 16, (EXT - ROWS) * 16)],
        dst_ref=spill,
        send_sem=spill_ssem,
        recv_sem=spill_rsem,
        device_id={"layer": g, "uvrow": after},
        device_id_type=MESH,
    )
    for chunk in range(CHUNKS):
        start = chunk * (SLOTS // 2)

        @pl.loop(start, start + SLOTS // 2, step=GROUP)
        def _(i):
            patches(i, GROUP)

        by_slot = jnp.transpose(tiles[...])[:16, : 3 * SLOTS]
        cos, sin = cos_sin_turns(by_slot * p0 * (1.0 / 16))
        mh, ml = halves(jnp.concatenate([cos, sin], axis=0))
        mix = jnp.where(exact, mh, ml)

        def tile_rows(first, last):
            @pl.loop(first, last, step=ROW_GROUP)
            def _(u):
                for n in range(ROW_GROUP):
                    tile_row(u + n, mix, chunk == 0)

        tile_rows(ROWS, EXT)
        if chunk == CHUNKS - 1:
            spill_copy.start()
        else:
            tile_rows(0, ROWS)

    for half in range(2):
        begin = (1 - half) * HALF
        tile_rows(begin, begin + HALF)
        if half == 1:
            spill_copy.wait()
            over = pl.ds(0, (EXT - ROWS) * 16)
            spec[:, over, :] = spec[:, over, :] + spill[...]

        for dx in range(4):
            there_x = (x + dx) & 3
            operand = []
            for i in range(4):
                place = pl.ds(begin * 16 + 4 * there_x + i, HALF, stride=16)
                re, im = spec[0, place, :], spec[1, place, :]
                operand.append(jnp.concatenate([re, -im], axis=1))
                operand.append(jnp.concatenate([im, re], axis=1))
            oh, ol = halves(jnp.concatenate(operand, axis=0))
            rows = lax.dot_general(
                outer[...], jnp.concatenate([oh, ol, oh], axis=1), NT, preferred_element_type=F32
            )
            for there_z in range(16):
                at = pl.multiple_of((4 * there_z + there_x) * 8, 8)
                col_send[half, pl.ds(at, 8), :] = rows[8 * there_z : 8 * there_z + 8]

            @pl.loop(0, 16 if dx else 15)
            def _(n):
                there = (((z - far_first(n, 16)) & 15) << 2) + there_x
                pltpu.make_async_remote_copy(
                    src_ref=col_send.at[half, pl.ds(pl.multiple_of(there * 8, 8), 8)],
                    dst_ref=col_recv.at[half, pl.ds(pl.multiple_of(w * 8, 8), 8)],
                    send_sem=col_ssem,
                    recv_sem=col_rsem.at[half],
                    device_id={"layer": g, "uvrow": there},
                    device_id_type=MESH,
                ).start()

    mine = pl.ds(pl.multiple_of(w * 8, 8), 8)
    for half in range(2):
        col_recv[half, mine, :] = col_send[half, mine, :]

    def arrived(half):
        others = col_recv.at[half, pl.ds(0, (BANDS - 1) * 8)]
        pltpu.make_async_copy(others, others, col_rsem.at[half]).wait()

    def half_image(half, first, count):
        held = jnp.concatenate(
            [col_recv[half, pl.ds(first + k, 64, stride=8), :] for k in range(count)], axis=1
        )
        hh, hl = halves(held)
        both = lax.dot_general(
            bands[...], jnp.concatenate([hh, hl, hh], axis=0), NN, preferred_element_type=F32
        )
        turned = []
        for k in range(count):
            a, b = both[:64, 128 * k : 128 * k + 128], both[64:, 128 * k : 128 * k + 128]
            turned.append(
                jnp.concatenate([a * turn[2 * half] - b * turn[2 * half + 1], a * turn[2 * half + 1] + b * turn[2 * half]], axis=1)
            )
        th, tl = halves(jnp.concatenate(turned, axis=0))
        return lax.dot_general(
            jnp.concatenate([th, tl, th], axis=1), final[half], NN, preferred_element_type=F32
        )

    arrived(0)
    for first in range(0, LAYERS, 4):
        partial[64 * first : 64 * first + 256, :] = half_image(0, first, 4)

    def red_copy(there):
        return pltpu.make_async_remote_copy(
            src_ref=red_send.at[there],
            dst_ref=red_recv.at[g],
            send_sem=red_ssem,
            recv_sem=red_rsem,
            device_id={"layer": there, "uvrow": w},
            device_id_type=MESH,
        )

    arrived(1)
    for step in range(2):
        first = ((g >> 2) ^ (1 - step)) * 4
        image = half_image(1, first, 4) + partial[pl.ds(pl.multiple_of(first * 64, 256), 256), :]
        for n in range(4):
            there = first + n
            piece = image[64 * n : 64 * n + 64]
            red_send[there] = piece[:, :128] * screen[there, 0] - piece[:, 128:] * screen[there, 1]

            @pl.when(there != g)
            def _():
                red_copy(there).start()

    red_recv[g] = red_send[g]
    others = red_recv.at[pl.ds(0, LAYERS - 1)]
    pltpu.make_async_copy(others, others, red_rsem).wait()
    total = red_recv[0]
    for layer in range(1, LAYERS):
        total = total + red_recv[layer]
    lines[...] = jnp.transpose(total)
    pairs[...] = jnp.concatenate([lines[pl.ds(n, 64, stride=2), :] for n in range(2)], axis=1)
    for n in range(16):
        out[:, 128 * n : 128 * n + 128] = pairs[pl.ds(n, 4, stride=16), :]

    sent = vis_send.at[pl.ds(0, (BANDS - 1) * 8)]
    pltpu.make_async_copy(sent, sent, vis_ssem).wait()
    sent = col_send.at[:, pl.ds(0, (BANDS - 1) * 8)]
    pltpu.make_async_copy(sent, sent, col_ssem).wait()
    sent = red_send.at[pl.ds(0, LAYERS - 1)]
    pltpu.make_async_copy(sent, sent, red_ssem).wait()

def per_device(vis_values, vis_cell, vis_offset, block_tile, block_band, layer_w):
    tables = [jnp.asarray(t) for t in host_tables()]
    operands = [
        vis_values, vis_cell, vis_offset, block_tile.reshape(1, BLOCKS), block_band.reshape(1, BLOCKS), layer_w, *tables,
    ]
    hbm = pl.BlockSpec(memory_space=pltpu.HBM)
    vmem = pl.BlockSpec(memory_space=pltpu.VMEM)
    dma = pltpu.SemaphoreType.DMA
    held = [(pltpu.SMEM if a is layer_w else pltpu.VMEM)(a.shape, a.dtype) for a in operands]
    return pl.pallas_call(
        kernel,
        out_shape=pltpu.VMEM((4, N), F32),
        in_specs=[hbm] * len(operands),
        out_specs=vmem,
        scratch_shapes=[
            *held,
            pltpu.VMEM((BANDS * 8, 128), F32),
            pltpu.VMEM((BANDS * 8, 128), F32),
            pltpu.VMEM((SLOTS * 2 * EXT, 128), F32),
            pltpu.VMEM((max(128, 3 * SLOTS), 128), F32),
            pltpu.VMEM((2, EXT * 16, 128), F32),
            pltpu.VMEM((2, (EXT - ROWS) * 16, 128), F32),
            pltpu.VMEM((2, BANDS * 8, 128), F32),
            pltpu.VMEM((2, BANDS * 8, 128), F32),
            pltpu.VMEM((LAYERS * 64, 256), F32),
            pltpu.VMEM((LAYERS, 2, 64, 128), F32),
            pltpu.VMEM((LAYERS, 64, 128), F32),
            pltpu.VMEM((LAYERS, 64, 128), F32),
            pltpu.VMEM((128, 64), F32),
            pltpu.VMEM((64, 128), F32),
            dma((len(operands),)), dma, dma((BANDS,)), dma, dma, dma, dma((2,)), dma, dma,
        ],
        compiler_params=pltpu.CompilerParams(
            collective_id=0, has_side_effects=True, vmem_limit_bytes=60 * 1024 * 1024
        ),
    )(*operands)

def solution(mesh):
    placed = (
        P(("layer", "uvrow"), None, None),
        P(("layer", "uvrow"), None),
        P(("layer", "uvrow"), None),
        P(("layer", "uvrow"), None),
        P(("layer", "uvrow"), None),
        P(),
    )
    return jax.shard_map(
        per_device,
        mesh=mesh,
        in_specs=placed,
        out_specs=P(("layer", "uvrow"), None),
        check_vma=False,
    )
```

```python
import functools
import math

import jax
import jax.numpy as jnp
import ml_dtypes
import numpy as np
from jax import lax
from jax.experimental import pallas as pl
from jax.experimental.pallas import tpu as pltpu
from jax.sharding import PartitionSpec as P

N = 2048
TW = 128
K = 8
OVS = 8
SPAN = TW - K + 1
BANDS = 64
LAYERS = 8
BLOCKS = 64
ROWS = 32
EXT = 40
OVER = K - 1
SIGMA = 1.45
WIDTH = 0.6
CHUNKS = 2
SLOTS = 2 * BANDS // CHUNKS
GROUP = 4
ROW_GROUP = 16
HALF = ROWS // 2
TAP_SCALE = math.sqrt(math.log2(math.e) / (2.0 * SIGMA * SIGMA))
MESH = pl.DeviceIdType.MESH
F32 = jnp.float32
BF16 = jnp.bfloat16
NN = (((1,), (0,)), ((), ()))
NT = (((1,), (1,)), ((), ()))

def far_first(n, count):
    return count // 2 + ((n + 1) >> 1) * (1 - 2 * (n & 1))

def near_first(n):
    return ((n + 2) >> 1) * (1 - 2 * (n & 1))

def halves(x):
    high = x.astype(BF16)
    low = (x - high.astype(F32)).astype(BF16)
    return high, low

def host_halves(x):
    high = x.astype(np.float32).astype(ml_dtypes.bfloat16)
    low = (x - high.astype(np.float64)).astype(np.float32).astype(ml_dtypes.bfloat16)
    return high, low

def host_tables():
    p1 = np.array([16 * k + z for z in range(16) for k in range(8)])
    col = np.arange(TW)
    angle = 2 * np.pi * ((p1[:, None] * col[None, :]) % TW) / TW
    high, low = host_halves(np.concatenate([np.cos(angle), np.sin(angle)], axis=1))
    outer = np.concatenate([high, high, low], axis=1)
    angle = 2 * np.pi * (np.arange(16)[:, None] * col[None, :]) / N
    twist = np.stack([np.cos(angle), np.sin(angle)]).astype(np.float32)
    q0 = np.arange(64)
    angle = 2 * np.pi * ((q0[:, None] * q0[None, :]) % 64) / 64
    high, low = host_halves(np.concatenate([np.cos(angle), np.sin(angle)], axis=0))
    bands = np.concatenate([high, high, low], axis=1)
    r = np.arange(ROWS)
    angle = 2 * np.pi * (q0[:, None] * r[None, :]) / N
    cos, sin = np.cos(angle), np.sin(angle)
    spans = [slice(HALF, ROWS), slice(0, HALF)]
    turn = np.stack(
        [
            np.concatenate([a[:, span], b[:, span]] * 4, axis=1)
            for span in spans
            for a, b in ((cos, -sin), (sin, cos))
        ]
    ).astype(np.float32)
    angle = 2 * np.pi * ((r[:, None] * r[None, :]) % ROWS) / ROWS
    cos, sin = np.cos(angle), np.sin(angle)
    last = np.zeros((2, 2, 4, 2, HALF, 2, 4, ROWS))
    for half in range(2):
        for i in range(4):
            for c in range(2):
                last[half, 0, i, c, :, 0, i, :] = cos[spans[half]]
                last[half, 0, i, c, :, 1, i, :] = sin[spans[half]]
                last[half, 1, i, c, :, 0, i, :] = -sin[spans[half]]
                last[half, 1, i, c, :, 1, i, :] = cos[spans[half]]
    high, low = host_halves(last.reshape(2, 256, 256))
    final = np.concatenate([high, high, low], axis=1)
    return outer, twist, bands, turn, final

def cos_sin_turns(turns):
    quarters = turns * 4.0
    whole = jnp.round(quarters)
    t = (quarters - whole) * (math.pi / 2)
    s = t * t
    sin = t + t * s * (-1.6666654611e-1 + s * (8.3321608736e-3 - s * 1.9515295891e-4))
    cos = 1.0 - 0.5 * s + s * s * (4.166664568298827e-2 + s * (-1.388731625493765e-3 + s * 2.443315711809948e-5))
    n = whole.astype(jnp.int32)
    odd = (n & 1) == 1
    a = jnp.where(odd, sin, cos)
    b = jnp.where(odd, cos, sin)
    a = jnp.where(((n + 1) & 2) == 2, -a, a)
    b = jnp.where((n & 2) == 2, -b, b)
    return a, b

def wrapped(pixel):
    return (((pixel + N // 2) & (N - 1)) - N // 2).astype(F32) * (WIDTH / N)

def kernel(
    values_hbm, cell_hbm, offset_hbm, tile_hbm, band_hbm, depth_hbm,
    outer_hbm, twist_hbm, bands_hbm, turn_hbm, final_hbm, out,
    values, cell, offset, tile, band, depth_ref, outer, twist, bands, turn, final,
    vis_send, vis_recv, parts, tiles, spec, spill, col_send, col_recv, partial, screen, red_send, red_recv, lines, pairs,
    load_sem, vis_ssem, vis_rsem, spill_ssem, spill_rsem, col_ssem, col_rsem, red_ssem, red_rsem,
):
    g, w = lax.axis_index("layer"), lax.axis_index("uvrow")
    z, x = w >> 2, w & 3

    barrier = pltpu.get_barrier_semaphore()
    loads = [
        pltpu.make_async_copy(there, here, load_sem.at[n])
        for n, (there, here) in enumerate(
            [
                (band_hbm, band), (tile_hbm, tile), (cell_hbm, cell), (offset_hbm, offset),
                (values_hbm, values), (depth_hbm, depth_ref), (twist_hbm, twist), (outer_hbm, outer),
                (bands_hbm, bands), (turn_hbm, turn), (final_hbm, final),
            ]
        )
    ]
    for load in loads:
        load.start()

    @pl.loop(0, BANDS - 1)
    def _(n):
        there = (w + far_first(n, BANDS)) & (BANDS - 1)
        pl.semaphore_signal(barrier, inc=1, device_id={"layer": g, "uvrow": there}, device_id_type=MESH)

    @pl.loop(1, LAYERS)
    def _(i):
        pl.semaphore_signal(barrier, inc=1, device_id={"layer": g ^ i, "uvrow": w}, device_id_type=MESH)

    for load in loads[:6]:
        load.wait()

    row_id = lax.broadcasted_iota(jnp.int32, (BLOCKS, BLOCKS), 0)
    col_id = lax.broadcasted_iota(jnp.int32, (BLOCKS, BLOCKS), 1)
    other = jnp.broadcast_to(band[...], (BLOCKS, BLOCKS))
    own = jnp.sum(jnp.where(row_id == col_id, other, 0), axis=1, keepdims=True)
    tile_of = jnp.sum(jnp.where(row_id == col_id, jnp.broadcast_to(tile[...], (BLOCKS, BLOCKS)), 0), axis=1, keepdims=True)
    same = own == other
    rank = jnp.sum(jnp.where(same & (row_id < col_id), 1, 0), axis=0, keepdims=True)
    cells = cell[...].astype(F32)
    rows = jnp.floor((cells + 0.5) * (1.0 / SPAN))
    cols = cells - rows * SPAN
    shifts = offset[...]
    u_place = rows * 8.0 + (shifts >> 3).astype(F32)
    v_place = (cols + tile_of.astype(F32) * TW) * 8.0 + (shifts & 7).astype(F32)
    data = jnp.concatenate([values[:, 0, :], values[:, 1, :], u_place, v_place], axis=1)
    first = data.astype(BF16)
    rest = data - first.astype(F32)
    second = rest.astype(BF16)
    third = (rest - second.astype(F32)).astype(BF16)
    stacked = jnp.concatenate([first, second, third], axis=0)
    for j in range(2):
        pick = jnp.where((row_id == other) & (rank == j), 1.0, 0.0).astype(BF16)
        pick = jnp.concatenate([pick, pick, pick], axis=1)
        slots = lax.dot_general(pick, stacked, NN, preferred_element_type=F32)
        for f in range(4):
            vis_send[pl.ds(4 * j + f, BANDS, stride=8), :] = slots[:, f * 128 : (f + 1) * 128]

    depth = depth_ref[g]
    lane = lax.broadcasted_iota(jnp.int32, (64, 128), 1)
    y = wrapped((lane & 31) * 64 + lax.broadcasted_iota(jnp.int32, (64, 128), 0))

    @pl.loop(0, LAYERS)
    def _(k):
        xp = wrapped(256 * k + 4 * w + (lane >> 5))
        r = xp * xp + y * y
        turns = depth * (-r / (1.0 + jnp.sqrt(1.0 - r)))
        cos, sin = cos_sin_turns(turns)
        screen[k, 0] = cos * (1.0 / N)
        screen[k, 1] = sin * (1.0 / N)

    pl.semaphore_wait(barrier, BANDS - 1 + LAYERS - 1)

    def vis_copy(there):
        return pltpu.make_async_remote_copy(
            src_ref=vis_send.at[pl.ds(pl.multiple_of(there * 8, 8), 8)],
            dst_ref=vis_recv.at[pl.ds(pl.multiple_of(w * 8, 8), 8)],
            send_sem=vis_ssem,
            recv_sem=vis_rsem.at[w],
            device_id={"layer": g, "uvrow": there},
            device_id_type=MESH,
        )

    @pl.loop(0, BANDS - 1)
    def _(n):
        vis_copy((w + near_first(n)) & (BANDS - 1)).start()

    mine = pl.ds(pl.multiple_of(w * 8, 8), 8)
    pltpu.make_async_copy(vis_send.at[mine], vis_recv.at[mine], vis_rsem.at[w]).start()
    for load in loads[6:]:
        load.wait()

    sublane = lax.broadcasted_iota(jnp.int32, (8, 128), 0)

    def source(n):
        return jnp.where(n == 0, w, (w - near_first(n - 1)) & (BANDS - 1))

    def taps(place):
        cell = place >> 3
        tap = (sublane - cell) & 7
        group = (cell + tap - sublane) >> 3
        far = (tap.astype(F32) - ((place & 7).astype(F32) * (1.0 / OVS) + (K - 1) / 2.0)) * TAP_SCALE
        return group, jnp.exp2(-(far * far))

    def spread(group, value, count):
        return jnp.concatenate([jnp.where(group == m, value, 0.0) for m in range(count)], axis=0)

    def split(value):
        high = value.astype(BF16).astype(F32)
        return high, value - high

    def patches(i, count):
        begins = [pl.multiple_of(source(i + n) * 8, 8) for n in range(count)]
        for n in range(count):
            piece = vis_recv.at[pl.ds(begins[n], 8)]
            pltpu.make_async_copy(piece, piece, vis_rsem.at[source(i + n)]).wait()
        for n in range(count):
            message = vis_recv[pl.ds(begins[n], 8), :]
            rows_high, rows_low, cols_high, cols_low = [], [], [], []
            for j in range(2):
                slot = (2 * (i + n) + j) & (SLOTS - 1)
                u_place = message[4 * j + 2 : 4 * j + 3].astype(jnp.int32)
                v_place = message[4 * j + 3 : 4 * j + 4].astype(jnp.int32)
                row_group, row_taps = taps(u_place)
                col_group, col_taps = taps(v_place & (TW * OVS - 1))
                re = split(row_taps * message[4 * j : 4 * j + 1])
                im = split(row_taps * message[4 * j + 1 : 4 * j + 2])
                cols = split(col_taps)
                wh, wl = [
                    jnp.concatenate(
                        [spread(row_group, re[p], EXT // 8), spread(row_group, im[p], EXT // 8)], axis=0
                    ).astype(BF16)
                    for p in range(2)
                ]
                ch, cl = [spread(col_group, cols[p], TW // 8).astype(BF16) for p in range(2)]
                rows_high.append(wh)
                rows_low.append(wl)
                cols_high.append(ch)
                cols_low.append(cl)
                number = (v_place >> 10).astype(F32)
                for copy in range(3):
                    tiles[pl.ds(copy * SLOTS + slot, 1), :] = number
            none = jnp.zeros((2 * EXT, 128), BF16)
            first = [jnp.concatenate([rows_high[0], none], axis=1), jnp.concatenate([none, rows_high[1]], axis=1)]
            low = lax.dot_general(
                jnp.concatenate(first, axis=0), jnp.concatenate(cols_low, axis=1), NT, preferred_element_type=F32
            )
            high = [lax.dot_general(jnp.concatenate([rows_high[j], rows_low[j]], axis=1), jnp.concatenate([cols_high[j], cols_high[j]], axis=1), NT, preferred_element_type=F32) for j in range(2)]
            patch = jnp.concatenate(high, axis=0) + low
            parts[pl.ds(pl.multiple_of(((2 * (i + n)) & (SLOTS - 1)) * 2 * EXT, 16), 4 * EXT), :] = patch

    p0 = lax.broadcasted_iota(jnp.int32, (16, 3 * SLOTS), 0).astype(F32)
    exact = lax.broadcasted_iota(jnp.int32, (32, 3 * SLOTS), 1) < 2 * SLOTS

    def tile_row(u, mix, begin):
        re = parts[pl.ds(u, SLOTS, stride=2 * EXT), :]
        im = parts[pl.ds(u + EXT, SLOTS, stride=2 * EXT), :]
        ph, plo = halves(jnp.concatenate([re, im], axis=1))
        both = lax.dot_general(
            mix, jnp.concatenate([ph, plo, ph], axis=0), NN, preferred_element_type=F32
        )
        re = both[:16, :128] - both[16:, 128:]
        im = both[:16, 128:] + both[16:, :128]
        tc, ts = twist[0], twist[1]
        at = pl.ds(u * 16 if isinstance(u, int) else pl.multiple_of(u * 16, 16), 16)
        new_re, new_im = re * tc - im * ts, re * ts + im * tc
        if begin:
            spec[0, at, :] = new_re
            spec[1, at, :] = new_im
        else:
            spec[0, at, :] += new_re
            spec[1, at, :] += new_im

    after = (w + 1) & (BANDS - 1)
    spill_copy = pltpu.make_async_remote_copy(
        src_ref=spec.at[:, pl.ds(ROWS * 16, OVER * 16)],
        dst_ref=spill,
        send_sem=spill_ssem,
        recv_sem=spill_rsem,
        device_id={"layer": g, "uvrow": after},
        device_id_type=MESH,
    )
    for chunk in range(CHUNKS):
        start = chunk * (SLOTS // 2)

        @pl.loop(start, start + SLOTS // 2, step=GROUP)
        def _(i):
            patches(i, GROUP)

        by_slot = jnp.transpose(tiles[...])[:16, : 3 * SLOTS]
        cos, sin = cos_sin_turns(by_slot * p0 * (1.0 / 16))
        mh, ml = halves(jnp.concatenate([cos, sin], axis=0))
        mix = jnp.where(exact, mh, ml)

        def tile_rows(first, last):
            @pl.loop(first, last, step=ROW_GROUP)
            def _(u):
                for n in range(ROW_GROUP):
                    tile_row(u + n, mix, chunk == 0)

        for u in range(ROWS, ROWS + OVER):
            tile_row(u, mix, chunk == 0)
        if chunk == CHUNKS - 1:
            spill_copy.start()
        else:
            tile_rows(0, ROWS)

    for half in range(2):
        begin = (1 - half) * HALF
        tile_rows(begin, begin + HALF)
        if half == 1:
            spill_copy.wait()
            over = pl.ds(0, OVER * 16)
            spec[:, over, :] = spec[:, over, :] + spill[...]

        for dx in range(4):
            there_x = (x + dx) & 3
            operand = []
            for i in range(4):
                place = pl.ds(begin * 16 + 4 * there_x + i, HALF, stride=16)
                re, im = spec[0, place, :], spec[1, place, :]
                operand.append(jnp.concatenate([re, -im], axis=1))
                operand.append(jnp.concatenate([im, re], axis=1))
            oh, ol = halves(jnp.concatenate(operand, axis=0))
            rows = lax.dot_general(
                outer[...], jnp.concatenate([oh, ol, oh], axis=1), NT, preferred_element_type=F32
            )
            for there_z in range(16):
                at = pl.multiple_of((4 * there_z + there_x) * 8, 8)
                col_send[half, pl.ds(at, 8), :] = rows[8 * there_z : 8 * there_z + 8]

            @pl.loop(0, 16 if dx else 15)
            def _(n):
                there = (((z - far_first(n, 16)) & 15) << 2) + there_x
                pltpu.make_async_remote_copy(
                    src_ref=col_send.at[half, pl.ds(pl.multiple_of(there * 8, 8), 8)],
                    dst_ref=col_recv.at[half, pl.ds(pl.multiple_of(w * 8, 8), 8)],
                    send_sem=col_ssem,
                    recv_sem=col_rsem.at[half],
                    device_id={"layer": g, "uvrow": there},
                    device_id_type=MESH,
                ).start()

    mine = pl.ds(pl.multiple_of(w * 8, 8), 8)
    for half in range(2):
        col_recv[half, mine, :] = col_send[half, mine, :]

    def arrived(half):
        others = col_recv.at[half, pl.ds(0, (BANDS - 1) * 8)]
        pltpu.make_async_copy(others, others, col_rsem.at[half]).wait()

    def half_image(half, first, count):
        held = jnp.concatenate(
            [col_recv[half, pl.ds(first + k, 64, stride=8), :] for k in range(count)], axis=1
        )
        hh, hl = halves(held)
        both = lax.dot_general(
            bands[...], jnp.concatenate([hh, hl, hh], axis=0), NN, preferred_element_type=F32
        )
        turned = []
        for k in range(count):
            a, b = both[:64, 128 * k : 128 * k + 128], both[64:, 128 * k : 128 * k + 128]
            turned.append(
                jnp.concatenate([a * turn[2 * half] - b * turn[2 * half + 1], a * turn[2 * half + 1] + b * turn[2 * half]], axis=1)
            )
        th, tl = halves(jnp.concatenate(turned, axis=0))
        return lax.dot_general(
            jnp.concatenate([th, tl, th], axis=1), final[half], NN, preferred_element_type=F32
        )

    arrived(0)
    for first in range(0, LAYERS, 4):
        partial[64 * first : 64 * first + 256, :] = half_image(0, first, 4)

    def red_copy(there):
        return pltpu.make_async_remote_copy(
            src_ref=red_send.at[there],
            dst_ref=red_recv.at[g],
            send_sem=red_ssem,
            recv_sem=red_rsem,
            device_id={"layer": there, "uvrow": w},
            device_id_type=MESH,
        )

    arrived(1)
    for step in range(2):
        first = ((g >> 2) ^ (1 - step)) * 4
        image = half_image(1, first, 4) + partial[pl.ds(pl.multiple_of(first * 64, 256), 256), :]
        for n in range(4):
            there = first + n
            piece = image[64 * n : 64 * n + 64]
            red_send[there] = piece[:, :128] * screen[there, 0] - piece[:, 128:] * screen[there, 1]

            @pl.when(there != g)
            def _():
                red_copy(there).start()

    red_recv[g] = red_send[g]
    others = red_recv.at[pl.ds(0, LAYERS - 1)]
    pltpu.make_async_copy(others, others, red_rsem).wait()
    total = red_recv[0]
    for layer in range(1, LAYERS):
        total = total + red_recv[layer]
    lines[...] = jnp.transpose(total)
    pairs[...] = jnp.concatenate([lines[pl.ds(n, 64, stride=2), :] for n in range(2)], axis=1)
    for n in range(16):
        out[:, 128 * n : 128 * n + 128] = pairs[pl.ds(n, 4, stride=16), :]

    sent = vis_send.at[pl.ds(0, (BANDS - 1) * 8)]
    pltpu.make_async_copy(sent, sent, vis_ssem).wait()
    sent = col_send.at[:, pl.ds(0, (BANDS - 1) * 8)]
    pltpu.make_async_copy(sent, sent, col_ssem).wait()
    sent = red_send.at[pl.ds(0, LAYERS - 1)]
    pltpu.make_async_copy(sent, sent, red_ssem).wait()

def per_device(vis_values, vis_cell, vis_offset, block_tile, block_band, layer_w):
    tables = [jnp.asarray(t) for t in host_tables()]
    operands = [
        vis_values, vis_cell, vis_offset, block_tile.reshape(1, BLOCKS), block_band.reshape(1, BLOCKS), layer_w, *tables,
    ]
    hbm = pl.BlockSpec(memory_space=pltpu.HBM)
    vmem = pl.BlockSpec(memory_space=pltpu.VMEM)
    dma = pltpu.SemaphoreType.DMA
    held = [(pltpu.SMEM if a is layer_w else pltpu.VMEM)(a.shape, a.dtype) for a in operands]
    return pl.pallas_call(
        kernel,
        out_shape=pltpu.VMEM((4, N), F32),
        in_specs=[hbm] * len(operands),
        out_specs=vmem,
        scratch_shapes=[
            *held,
            pltpu.VMEM((BANDS * 8, 128), F32),
            pltpu.VMEM((BANDS * 8, 128), F32),
            pltpu.VMEM((SLOTS * 2 * EXT, 128), F32),
            pltpu.VMEM((max(128, 3 * SLOTS), 128), F32),
            pltpu.VMEM((2, EXT * 16, 128), F32),
            pltpu.VMEM((2, OVER * 16, 128), F32),
            pltpu.VMEM((2, BANDS * 8, 128), F32),
            pltpu.VMEM((2, BANDS * 8, 128), F32),
            pltpu.VMEM((LAYERS * 64, 256), F32),
            pltpu.VMEM((LAYERS, 2, 64, 128), F32),
            pltpu.VMEM((LAYERS, 64, 128), F32),
            pltpu.VMEM((LAYERS, 64, 128), F32),
            pltpu.VMEM((128, 64), F32),
            pltpu.VMEM((64, 128), F32),
            dma((len(operands),)), dma, dma((BANDS,)), dma, dma, dma, dma((2,)), dma, dma,
        ],
        compiler_params=pltpu.CompilerParams(
            collective_id=0, has_side_effects=True, vmem_limit_bytes=60 * 1024 * 1024
        ),
    )(*operands)

def solution(mesh):
    placed = (
        P(("layer", "uvrow"), None, None),
        P(("layer", "uvrow"), None),
        P(("layer", "uvrow"), None),
        P(("layer", "uvrow"), None),
        P(("layer", "uvrow"), None),
        P(),
    )
    return jax.shard_map(
        per_device,
        mesh=mesh,
        in_specs=placed,
        out_specs=P(("layer", "uvrow"), None),
        check_vma=False,
    )
```
